32 devices in a mesh: su: 8 (over z, core), sv: 2 (over x), nrm: 2 (over y).
Axes of the slice: x: 2, y: 2, z: 4, core: 2. Of those that a mesh axis runs over, the one named last changes fastest.
Arguments:
- primitive: float32 [5, 128, 80, 256], P(None, 'su', 'sv', 'nrm'), may hold values from -4 to 4, as said below
- adjoint_state: float32 [5, 128, 80, 256], P(None, 'su', 'sv', 'nrm'), may hold values from -0.6 to 0.6
- objective_grad: float32 [5, 128, 80, 256], P(None, 'su', 'sv', 'nrm'), may hold values from -6 to 6
- front_height: float32 [128, 80], P('su', 'sv'), may hold values from 0.8 to 1.25
- shock_state: float32 [5, 128, 80], P(None, 'su', 'sv'), may hold values from -4 to 4, as said below
- state_by_height: float32 [5, 128, 80], P(None, 'su', 'sv'), may hold values from -18 to 18
- state_by_slope: float32 [5, 128, 80], P(None, 'su', 'sv'), may hold values from -6 to 6
- fitted_flags: int32 [128, 80], P('su', 'sv'), may hold values 0 or 1
Outputs:
- adjoint_residual: float32 [5, 128, 80, 256], P(None, 'su', 'sv', 'nrm')
- slope_sensitivity: float32 [128, 80], P('su', 'sv')
The draws below stay inside these ranges and needn't reach their ends.
Inputs may be any that keep to these rules, and one draw needn't show every extreme that they name: `primitive`: variables 0 (density) and 4 (pressure) lie in 0.5 to 2; variables 1 to 3 are velocity components. `shock_state`: variables 0 (density) and 4 (pressure) lie in 0.5 to 2; variables 1 to 3 are velocity components.
All inputs are finite; a program needn't handle non-finite values. No bound on the sum of `fitted_flags` on one device may be relied on, other than what follows from the above.
Results may differ from the reference program's by a relative error of at most 0.0003.
Values sent between devices are 32-bit elements; how exact they have to be, the bound alone decides.
A program may use at most 128 MiB of HBM per device.

```python
import jax
import jax.numpy as jnp
from jax import lax

CU = 16
NU = 128
NV = 80
NN = 256
N_SU = 8


def primitive_fields(key, shape):
    subkeys = jax.random.split(key, 3)
    density = jax.random.uniform(subkeys[0], shape, jnp.float32, 0.5, 2.0)
    pressure = jax.random.uniform(subkeys[2], shape, jnp.float32, 0.5, 2.0)
    velocity = jnp.clip(1.5 * jax.random.normal(subkeys[1], (3,) + shape, jnp.float32), -4.0, 4.0)
    return jnp.concatenate([density[None], velocity, pressure[None]], 0)


def draw_primitive(key, part):
    return primitive_fields(key, (NU, NV, NN))


def draw_shock_state(key, part):
    return primitive_fields(jax.random.fold_in(key, 7), (NU, NV))


def set_ends(entries, key, least, largest):
    longest = entries.shape.index(max(entries.shape))
    spots = []
    for shift in (0, 1):
        where = [jax.random.randint(jax.random.fold_in(key, axis), (), 0, length) for axis, length in enumerate(entries.shape)]
        where[longest] = (where[longest] + shift) % entries.shape[longest]
        spots.append(tuple(where))
    return entries.at[spots[0]].set(least).at[spots[1]].set(largest)


def level_of(rng, extent, cuts, low, high):
    gain, own = 1.0, jax.random.fold_in(rng, 6)
    for dim, parts in cuts:
        heights = jnp.exp(jax.random.uniform(jax.random.fold_in(own, dim), (parts,), jnp.float32, low / len(cuts), high / len(cuts)))
        gain = gain * jnp.repeat(heights, extent[dim] // parts).reshape([-1 if axis == dim else 1 for axis in range(len(extent))])
    return gain


def centred(key, shape, width, bound, cuts=(), kind=jnp.bfloat16):
    drawn = width * jax.random.normal(key, shape, jnp.float32)
    if cuts:
        drawn = drawn * level_of(key, shape, cuts, -0.22, 0.18)
    return jnp.clip(drawn, -bound, bound).astype(kind)


def setup_inputs(seed: int = 0) -> dict:
    keys = jax.random.split(jax.random.key(seed), 9)
    return {
        "primitive": draw_primitive(jax.random.fold_in(keys[8], 71), 0),
        "adjoint_state": centred(keys[1], (5, NU, NV, NN), 0.1, 0.6, ((1, 8), (2, 2), (3, 2)), jnp.float32),
        "objective_grad": centred(keys[2], (5, NU, NV, NN), 1.0, 6.0, ((1, 8), (2, 2), (3, 2)), jnp.float32),
        "front_height": jnp.clip(0.8 + 0.45 * jax.random.uniform(keys[3], (NU, NV), jnp.float32) ** level_of(keys[3], (NU, NV), ((0, 8), (1, 2)), -0.2, 0.2), 0.8, 1.25),
        "shock_state": draw_shock_state(jax.random.fold_in(keys[8], 71), 0),
        "state_by_height": centred(keys[5], (5, NU, NV), 3.0, 18.0, ((1, 8), (2, 2)), jnp.float32),
        "state_by_slope": centred(keys[6], (5, NU, NV), 1.0, 6.0, ((1, 8), (2, 2)), jnp.float32),
        "fitted_flags": set_ends((jax.random.randint(keys[7], (NU, NV), 0, 4) < 3).astype(jnp.int32), jax.random.fold_in(keys[7], 1), 0, 1),
    }


gamma_ratio = 1.4
damping_coef = 0.0625
stretch_rate = 2.2

def thermo(state):
    speed_square = state[1] * state[1] + state[2] * state[2] + state[3] * state[3]
    kinetic = 0.5 * (gamma_ratio - 1.0) * speed_square
    enthalpy = gamma_ratio * state[4] / ((gamma_ratio - 1.0) * state[0]) + 0.5 * speed_square
    return (kinetic, enthalpy)

def line_flux(state, enthalpy):
    mass_flow = state[0] * state[3]
    return jnp.stack([mass_flow, mass_flow * state[1], mass_flow * state[2], mass_flow * state[3] + state[4], mass_flow * enthalpy], 0)

def flux_transpose(state, kinetic, enthalpy, adjoint, direction):
    normal_speed = state[direction]
    projected = adjoint[direction]
    dotted = state[1] * adjoint[1] + state[2] * adjoint[2] + state[3] * adjoint[3]
    energy_term = adjoint[4]
    mass_row = kinetic * projected - normal_speed * dotted + normal_speed * (kinetic - enthalpy) * energy_term
    common = adjoint[0] + dotted + enthalpy * energy_term
    shared = projected + normal_speed * energy_term
    pieces = [mass_row]
    for component in (1, 2, 3):
        entry = normal_speed * adjoint[component] - (gamma_ratio - 1.0) * state[component] * shared
        if component == direction:
            entry = entry + common
        pieces.append(entry)
    pieces.append((gamma_ratio - 1.0) * projected + gamma_ratio * normal_speed * energy_term)
    return jnp.stack(pieces, 0)

def tangent_parts(padded_adjoint, padded_radius, along_axis, length):

    def window(source, offset):
        return lax.slice_in_dim(source, offset, offset + length, axis=along_axis)
    gradient = (8.0 * (window(padded_adjoint, 1) - window(padded_adjoint, 3)) - (window(padded_adjoint, 0) - window(padded_adjoint, 4))) / 12.0
    weighted = padded_radius[None] * padded_adjoint
    fourth = window(weighted, 0) - 4.0 * window(weighted, 1) + 6.0 * window(weighted, 2) - 4.0 * window(weighted, 3) + window(weighted, 4)
    return (gradient, fourth)

def reference(primitive, adjoint_state, objective_grad, front_height, shock_state, state_by_height, state_by_slope, fitted_flags):
    fraction = (jnp.arange(NN).astype(jnp.float32) + 0.5) / NN
    stretch = jnp.exp(stretch_rate * (fraction - 1.0))
    sound_speed = jnp.sqrt(gamma_ratio * primitive[4] / primitive[0])
    radius_first = jnp.abs(primitive[1]) + sound_speed
    padded_adjoint = jnp.pad(adjoint_state, ((0, 0), (2, 2), (0, 0), (0, 0)))
    padded_radius = jnp.pad(radius_first, ((2, 2), (0, 0), (0, 0)))
    shock_kinetic, shock_enthalpy = thermo(shock_state)
    shock_flux = line_flux(shock_state, shock_enthalpy)

    def block_terms(block_index):
        first_row = (block_index * CU).astype(jnp.int32)
        adjoint_rows = lax.dynamic_slice_in_dim(padded_adjoint, first_row, CU + 4, 1)
        radius_rows = lax.dynamic_slice_in_dim(padded_radius, first_row, CU + 4, 0)
        state = lax.dynamic_slice_in_dim(primitive, first_row, CU, 1)
        target = lax.dynamic_slice_in_dim(objective_grad, first_row, CU, 1)
        height = lax.dynamic_slice_in_dim(front_height, first_row, CU, 0)
        shock = lax.dynamic_slice_in_dim(shock_state, first_row, CU, 1)
        shock_kin = lax.dynamic_slice_in_dim(shock_kinetic, first_row, CU, 0)
        shock_enth = lax.dynamic_slice_in_dim(shock_enthalpy, first_row, CU, 0)
        flux_top = lax.dynamic_slice_in_dim(shock_flux, first_row, CU, 1)
        kinetic, enthalpy = thermo(state)
        center = adjoint_rows[:, 2:CU + 2]
        first_grad, first_fourth = tangent_parts(adjoint_rows, radius_rows, 1, CU)
        radius_second = jnp.abs(state[2]) + jnp.sqrt(gamma_ratio * state[4] / state[0])
        second_grad, second_fourth = tangent_parts(jnp.pad(center, ((0, 0), (0, 0), (2, 2), (0, 0))), jnp.pad(radius_second, ((0, 0), (2, 2), (0, 0))), 2, NV)
        scaled = center / (2.0 * height[None, :, :, None] * stretch[None, None, None, :])
        padded_scaled = jnp.pad(scaled, ((0, 0), (0, 0), (0, 0), (1, 1)))
        fluxes = line_flux(state, enthalpy)
        flux_above = jnp.concatenate([fluxes[..., 1:], flux_top[..., None]], -1)
        flux_below = jnp.concatenate([jnp.zeros_like(fluxes[..., :1]), fluxes[..., :-1]], -1)
        metric = -lax.optimization_barrier(jnp.sum(scaled * (flux_above - flux_below), axis=(0, 3))) / height
        shock_adjoint = flux_transpose(shock, shock_kin, shock_enth, scaled[..., -1], 3)
        residual = target + flux_transpose(state, kinetic, enthalpy, first_grad, 1) + flux_transpose(state, kinetic, enthalpy, second_grad, 2) + damping_coef * (first_fourth + second_fourth) + flux_transpose(state, kinetic, enthalpy, padded_scaled[..., :-2] - padded_scaled[..., 2:], 3)
        return (residual, metric, shock_adjoint)
    residual_blocks, metric_blocks, shock_blocks = lax.map(block_terms, jnp.arange(N_SU, dtype=jnp.int32))
    residual = jnp.moveaxis(residual_blocks, 0, 1).reshape(5, NU, NV, NN)
    metric = metric_blocks.reshape(NU, NV)
    shock_adjoint = jnp.moveaxis(shock_blocks, 0, 1).reshape(5, NU, NV)
    fitted = fitted_flags.astype(jnp.float32)
    height_term = metric + fitted * lax.optimization_barrier(jnp.sum(shock_adjoint * state_by_height, 0))
    slope_sensitivity = lax.cumsum(height_term, axis=0, reverse=True) / NU + fitted * lax.optimization_barrier(jnp.sum(shock_adjoint * state_by_slope, 0))
    enthalpy_all = thermo(primitive)[1]
    adjoint_residual = residual + fraction[None, None, None, :] * slope_sensitivity[None, :, :, None] * line_flux(primitive, enthalpy_all)
    return (adjoint_residual, slope_sensitivity)
```

```python
import functools
import math

import jax
import jax.numpy as jnp
from jax import lax
from jax.experimental import pallas as pl
from jax.experimental.pallas import tpu as pltpu
from jax.sharding import PartitionSpec as P

gamma_ratio = 1.4
gamma_less = gamma_ratio - 1.0
damping_coef = 0.0625
stretch_rate = 2.2
MESH = pl.DeviceIdType.MESH
SUB = 8
LANES = 128


def thermo(state):
    speed_square = state[1] * state[1] + state[2] * state[2] + state[3] * state[3]
    kinetic = 0.5 * gamma_less * speed_square
    enthalpy = gamma_ratio * state[4] / (gamma_less * state[0]) + 0.5 * speed_square
    return (kinetic, enthalpy)


def line_flux(state, enthalpy):
    mass_flow = state[0] * state[3]
    return [
        mass_flow,
        mass_flow * state[1],
        mass_flow * state[2],
        mass_flow * state[3] + state[4],
        mass_flow * enthalpy,
    ]


def flux_transpose_normal(state, kinetic, enthalpy, adjoint):
    normal_speed = state[3]
    projected = adjoint[3]
    dotted = state[1] * adjoint[1] + state[2] * adjoint[2] + state[3] * adjoint[3]
    energy_term = adjoint[4]
    mass_row = (
        kinetic * projected
        - normal_speed * dotted
        + normal_speed * (kinetic - enthalpy) * energy_term
    )
    common = adjoint[0] + dotted + enthalpy * energy_term
    shared = projected + normal_speed * energy_term
    pieces = [mass_row]
    for component in (1, 2, 3):
        entry = normal_speed * adjoint[component] - gamma_less * state[component] * shared
        if component == 3:
            entry = entry + common
        pieces.append(entry)
    pieces.append(gamma_less * projected + gamma_ratio * normal_speed * energy_term)
    return pieces


def kernel(
    n_su, n_sv,
    height_ref, shock_ref, by_height_ref, by_slope_ref, fitted_ref,
    prim_hbm, psi_hbm, obj_hbm,
    out_hbm, slope_ref,
    psi, prim, out, normal, enth, rad_u, rad_v,
    sv_send, sv_recv, edge_send, edge_recv, top_pack, turn, height_t, slope_t,
    half_send, half_recv, tot_send, tot_recv,
    load_sem, store_sem, send_sem, recv_sem, tot_ssem, tot_rsem,
):
    rows, cols = prim.shape[1], prim.shape[2]
    chunks = cols // SUB
    su, sv, nrm = lax.axis_index("su"), lax.axis_index("sv"), lax.axis_index("nrm")
    own = pl.ds(SUB, cols)

    load_psi = pltpu.make_async_copy(psi_hbm, psi.at[:, pl.ds(2, rows), own], load_sem.at[0])
    load_prim = pltpu.make_async_copy(prim_hbm, prim, load_sem.at[1])
    load_obj = pltpu.make_async_copy(obj_hbm, out, load_sem.at[2])
    load_psi.start()
    load_prim.start()
    load_obj.start()

    barrier = pltpu.get_barrier_semaphore()
    for step in range(1, n_su):
        pl.semaphore_signal(
            barrier, inc=1, device_id={"su": lax.rem(su + step, n_su)}, device_id_type=MESH
        )
    pl.semaphore_signal(barrier, inc=1, device_id={"nrm": 1 - nrm}, device_id_type=MESH)

    @pl.when(sv > 0)
    def _():
        pl.semaphore_signal(barrier, inc=1, device_id={"sv": sv - 1}, device_id_type=MESH)

    @pl.when(sv < n_sv - 1)
    def _():
        pl.semaphore_signal(barrier, inc=1, device_id={"sv": sv + 1}, device_id_type=MESH)

    def remote(src, dst, slot, where):
        return pltpu.make_async_remote_copy(
            src_ref=src,
            dst_ref=dst,
            send_sem=send_sem.at[slot],
            recv_sem=recv_sem.at[slot],
            device_id=where,
            device_id_type=MESH,
        )

    psi_down = remote(
        psi_hbm.at[:, pl.ds(0, 2)], psi.at[:, pl.ds(rows + 2, 2), own], 0, {"su": su - 1}
    )
    psi_up = remote(
        psi_hbm.at[:, pl.ds(rows - 2, 2)], psi.at[:, pl.ds(0, 2), own], 1, {"su": su + 1}
    )
    rad_down = remote(rad_u.at[pl.ds(2, 2)], rad_u.at[pl.ds(rows + 2, 2)], 2, {"su": su - 1})
    rad_up = remote(rad_u.at[pl.ds(rows, 2)], rad_u.at[pl.ds(0, 2)], 3, {"su": su + 1})
    sv_down = remote(sv_send.at[0], sv_recv.at[1], 4, {"sv": sv - 1})
    sv_up = remote(sv_send.at[1], sv_recv.at[0], 5, {"sv": sv + 1})
    edge = remote(edge_send, edge_recv, 6, {"nrm": 1 - nrm})
    half = remote(half_send, half_recv, 7, {"nrm": 1 - nrm})

    lane = lax.broadcasted_iota(jnp.int32, (1, LANES), 1)
    total_depth = 2 * LANES
    place = (nrm * LANES + lane).astype(jnp.float32)
    fraction = (place + 0.5) / total_depth

    def half_inverse(position):
        return 0.5 * jnp.exp(stretch_rate * (1.0 - (position + 0.5) / total_depth))

    below = jnp.where(lane == 0, 0.0, half_inverse(place - 1.0))
    above = jnp.where(lane == LANES - 1, 0.0, half_inverse(place + 1.0))
    target = jnp.where(nrm == 0, LANES - 1, 0)
    edge_weight = jnp.where(
        lane == target,
        jnp.where(nrm == 0, -half_inverse(place + 1.0), half_inverse(place - 1.0)),
        0.0,
    )

    turn[...] = jnp.zeros_like(turn)
    turn[0:rows, 0:cols] = 1.0 / height_ref[...]
    height_t[...] = turn[...].T[0:cols]

    @pl.when(su == 0)
    def _():
        psi[:, 0:2, SUB : SUB + cols] = jnp.zeros((5, 2, cols, LANES), jnp.float32)
        rad_u[0:2] = jnp.zeros((2, cols, LANES), jnp.float32)

    @pl.when(su == n_su - 1)
    def _():
        psi[:, rows + 2 : rows + 4, SUB : SUB + cols] = jnp.zeros((5, 2, cols, LANES), jnp.float32)
        rad_u[rows + 2 : rows + 4] = jnp.zeros((2, cols, LANES), jnp.float32)

    @pl.when(sv == 0)
    def _():
        sv_recv[0] = jnp.zeros((6, rows, 2, LANES), jnp.float32)

    @pl.when(sv == n_sv - 1)
    def _():
        sv_recv[1] = jnp.zeros((6, rows, 2, LANES), jnp.float32)

    neighbours = n_su + (sv > 0).astype(jnp.int32) + (sv < n_sv - 1).astype(jnp.int32)
    pl.semaphore_wait(barrier, neighbours)

    @pl.when(su > 0)
    def _():
        psi_down.start()

    @pl.when(su < n_su - 1)
    def _():
        psi_up.start()

    load_psi.wait()

    def pack(row, carry):
        top, bottom = carry
        for comp in range(5):
            spot = comp * rows + row
            rolled = pltpu.roll(psi[comp, row + 2, SUB : SUB + cols, :], spot + 1, 1)
            top = jnp.where(lane == spot, rolled, top)
            bottom = jnp.where(lane == spot + 1, rolled, bottom)
        return (top, bottom)

    blank = jnp.zeros((cols, LANES), jnp.float32)
    top, bottom = lax.fori_loop(0, rows, pack, (blank, blank))
    top_pack[...] = top
    edge_send[...] = jnp.where(nrm == 0, top, pltpu.roll(bottom, LANES - 1, 1))
    edge.start()

    load_prim.wait()

    def radii(row, carry):
        for chunk in range(chunks):
            part = slice(chunk * SUB, chunk * SUB + SUB)
            state = [prim[comp, row, part, :] for comp in range(5)]
            square = gamma_ratio * state[4] / state[0]
            sound = jnp.sqrt(square)
            speed_square = state[1] * state[1] + state[2] * state[2] + state[3] * state[3]
            enth[row, part, :] = square * (1.0 / gamma_less) + 0.5 * speed_square
            rad_u[row + 2, part, :] = damping_coef * (jnp.abs(state[1]) + sound)
            rad_v[row, SUB + chunk * SUB : 2 * SUB + chunk * SUB, :] = damping_coef * (
                jnp.abs(state[2]) + sound
            )
        for comp in range(5):
            sv_send[0, comp, row] = psi[comp, row + 2, SUB : SUB + 2, :]
            sv_send[1, comp, row] = psi[comp, row + 2, SUB + cols - 2 : SUB + cols, :]
        sv_send[0, 5, row] = rad_v[row, SUB : SUB + 2, :]
        sv_send[1, 5, row] = rad_v[row, SUB + cols - 2 : SUB + cols, :]
        return carry

    lax.fori_loop(0, rows, radii, 0)

    @pl.when(sv > 0)
    def _():
        sv_down.start()

    @pl.when(sv < n_sv - 1)
    def _():
        sv_up.start()

    @pl.when(su > 0)
    def _():
        rad_down.start()

    @pl.when(su < n_su - 1)
    def _():
        rad_up.start()

    edge.wait_recv()

    def metric_row(row, sums):
        scale = pltpu.roll(height_t[...], LANES - row, 1)[:, 0:1]
        pieces = []
        for chunk in range(chunks):
            part = slice(chunk * SUB, chunk * SUB + SUB)
            state = [prim[comp, row, part, :] for comp in range(5)]
            flux = line_flux(state, enth[row, part, :])
            factor = jnp.broadcast_to(scale[part], (SUB, LANES))
            total = None
            for comp in range(5):
                value = psi[comp, row + 2, SUB + chunk * SUB : 2 * SUB + chunk * SUB, :]
                shift = lax.rem(target - (comp * rows + row) + LANES, LANES)
                difference = (
                    pltpu.roll(value, 1, 1) * below
                    - pltpu.roll(value, LANES - 1, 1) * above
                    + pltpu.roll(edge_recv[part, :], shift, 1) * edge_weight
                ) * factor
                normal[comp, row, part, :] = difference
                term = flux[comp] * difference
                total = term if total is None else total + term
            pieces.append(jnp.sum(total, axis=1, keepdims=True))
        return jnp.where(lane == row, jnp.concatenate(pieces, 0), sums)

    sums = lax.fori_loop(0, rows, metric_row, blank)

    turn[...] = jnp.zeros_like(turn)
    turn[0:cols, :] = sums
    line_sums = turn[...].T[0:rows, 0:cols]
    turn[0:cols, :] = top_pack[...]
    tops = turn[...].T
    inverse = 1.0 / height_ref[...]
    last = 0.5 * math.exp(stretch_rate * 0.5 / total_depth)
    top_scaled = [
        tops[comp * rows : comp * rows + rows, 0:cols] * (last * inverse) for comp in range(5)
    ]
    shock = [shock_ref[comp] for comp in range(5)]
    shock_kinetic, shock_enthalpy = thermo(shock)
    shock_flux = line_flux(shock, shock_enthalpy)
    shock_adjoint = flux_transpose_normal(shock, shock_kinetic, shock_enthalpy, top_scaled)
    fitted = fitted_ref[...].astype(jnp.float32)
    front_flux = sum(top_scaled[comp] * shock_flux[comp] for comp in range(5))
    front_height = fitted * sum(shock_adjoint[comp] * by_height_ref[comp] for comp in range(5))
    front_slope = fitted * sum(shock_adjoint[comp] * by_slope_ref[comp] for comp in range(5))
    on_front = nrm == 1
    half_send[...] = jnp.zeros_like(half_send)
    half_send[0, :, 0:cols] = (
        jnp.where(on_front, front_height - front_flux * inverse, 0.0) - line_sums * inverse
    )
    half_send[1, :, 0:cols] = jnp.where(on_front, front_slope, 0.0)
    half.start()

    @pl.when(sv > 0)
    def _():
        sv_up.wait_recv()

    @pl.when(sv < n_sv - 1)
    def _():
        sv_down.wait_recv()

    def unpack(row, carry):
        for comp in range(5):
            psi[comp, row + 2, SUB - 2 : SUB, :] = sv_recv[0, comp, row]
            psi[comp, row + 2, SUB + cols : SUB + cols + 2, :] = sv_recv[1, comp, row]
        rad_v[row, SUB - 2 : SUB, :] = sv_recv[0, 5, row]
        rad_v[row, SUB + cols : SUB + cols + 2, :] = sv_recv[1, 5, row]
        return carry

    lax.fori_loop(0, rows, unpack, 0)
    load_obj.wait()

    def residual_row(row, carry):
        for chunk in range(chunks):
            first = chunk * SUB
            part = slice(first, first + SUB)
            wide = slice(SUB + first, 2 * SUB + first)
            density, u1, u2, u3, pressure = [prim[comp, row, part, :] for comp in range(5)]
            enthalpy = enth[row, part, :]
            ru = [rad_u[row + offset, part, :] for offset in range(5)]
            rv = [rad_v[row, wide.start + offset - 2 : wide.stop + offset - 2, :] for offset in range(5)]
            ruv = 6.0 * (ru[2] + rv[2])
            g1, g2, damped = [], [], []
            for comp in range(5):
                centre = psi[comp, row + 2, wide, :]
                along = [psi[comp, row + offset, wide, :] for offset in (0, 1, 3, 4)]
                across = [
                    psi[comp, row + 2, wide.start + offset : wide.stop + offset, :]
                    for offset in (-2, -1, 1, 2)
                ]
                g1.append((along[1] - along[2]) * (2.0 / 3.0) - (along[0] - along[3]) * (1.0 / 12.0))
                g2.append((across[1] - across[2]) * (2.0 / 3.0) - (across[0] - across[3]) * (1.0 / 12.0))
                far = ru[0] * along[0] + ru[4] * along[3] + rv[0] * across[0] + rv[4] * across[3]
                near = ru[1] * along[1] + ru[3] * along[2] + rv[1] * across[1] + rv[3] * across[2]
                damped.append(far - 4.0 * near + ruv * centre)
            g3 = [normal[comp, row, part, :] for comp in range(5)]
            kinetic = (0.5 * gamma_less) * (u1 * u1 + u2 * u2 + u3 * u3)
            speeds = (u1, u2, u3)
            grads = (g1, g2, g3)
            spread = g1[1] + g2[2] + g3[3]
            energy = u1 * g1[4] + u2 * g2[4] + u3 * g3[4]
            carried = [u1 * g1[b] + u2 * g2[b] + u3 * g3[b] for b in (1, 2, 3)]
            shared = gamma_less * (spread + energy)
            out[0, row, part, :] = (
                out[0, row, part, :]
                + damped[0]
                + kinetic * spread
                - (u1 * carried[0] + u2 * carried[1] + u3 * carried[2])
                + (kinetic - enthalpy) * energy
            )
            for b in (1, 2, 3):
                g = grads[b - 1]
                dotted = u1 * g[1] + u2 * g[2] + u3 * g[3]
                out[b, row, part, :] = (
                    out[b, row, part, :]
                    + damped[b]
                    + carried[b - 1]
                    - speeds[b - 1] * shared
                    + (g[0] + dotted + enthalpy * g[4])
                )
            out[4, row, part, :] = (
                out[4, row, part, :] + damped[4] + gamma_less * spread + gamma_ratio * energy
            )
        return carry

    middle = rows // 2
    lax.fori_loop(2, middle, residual_row, 0)

    half.wait_recv()
    summed = half_send[0, :, 0:cols] + half_recv[0, :, 0:cols]
    front_slope = half_send[1, :, 0:cols] + half_recv[1, :, 0:cols]
    step = 1
    while step < rows:
        summed = summed + jnp.concatenate(
            [summed[step:], jnp.zeros((step, cols), jnp.float32)], 0
        )
        step *= 2
    tot_send[...] = jnp.zeros_like(tot_send)
    tot_send[:, 0:cols] = summed[0:1]

    def total_copy(source, dest):
        return pltpu.make_async_remote_copy(
            src_ref=tot_send,
            dst_ref=tot_recv.at[source],
            send_sem=tot_ssem.at[dest],
            recv_sem=tot_rsem.at[source],
            device_id={"su": dest},
            device_id_type=MESH,
        )

    for other in range(n_su - 1):
        @pl.when(other < su)
        def _(other=other):
            total_copy(su, other).start()

    lax.fori_loop(middle, rows - 2, residual_row, 0)

    @pl.when(su > 0)
    def _():
        psi_up.wait_recv()
        rad_up.wait_recv()

    @pl.when(su < n_su - 1)
    def _():
        psi_down.wait_recv()
        rad_down.wait_recv()

    lax.fori_loop(0, 2, residual_row, 0)
    lax.fori_loop(rows - 2, rows, residual_row, 0)

    for other in range(1, n_su):
        @pl.when(other > su)
        def _(other=other):
            total_copy(other, su).wait_recv()

    upstream = jnp.zeros((1, cols), jnp.float32)
    for other in range(n_su - 1, 0, -1):
        upstream = upstream + jnp.where(other > su, tot_recv[other, :, 0:cols], 0.0)
    slope = (summed + upstream) * (1.0 / (rows * n_su)) + front_slope
    slope_ref[...] = slope
    turn[...] = jnp.zeros_like(turn)
    turn[0:rows, 0:cols] = slope
    slope_t[...] = turn[...].T[0:cols]

    def store(row):
        return pltpu.make_async_copy(
            out.at[:, pl.ds(row, 1)], out_hbm.at[:, pl.ds(row, 1)], store_sem.at[row]
        )

    def slope_row(row, carry):
        column = pltpu.roll(slope_t[...], LANES - row, 1)[:, 0:1]
        for chunk in range(chunks):
            part = slice(chunk * SUB, chunk * SUB + SUB)
            state = [prim[comp, row, part, :] for comp in range(5)]
            flux = line_flux(state, enth[row, part, :])
            weight = jnp.broadcast_to(column[part], (SUB, LANES)) * fraction
            for comp in range(5):
                out[comp, row, part, :] = out[comp, row, part, :] + weight * flux[comp]
        store(row).start()
        return carry

    lax.fori_loop(0, rows, slope_row, 0)

    @pl.when(su > 0)
    def _():
        psi_down.wait_send()
        rad_down.wait_send()

    @pl.when(su < n_su - 1)
    def _():
        psi_up.wait_send()
        rad_up.wait_send()

    @pl.when(sv > 0)
    def _():
        sv_down.wait_send()

    @pl.when(sv < n_sv - 1)
    def _():
        sv_up.wait_send()

    edge.wait_send()
    half.wait_send()
    for other in range(n_su - 1):
        @pl.when(other < su)
        def _(other=other):
            total_copy(su, other).wait_send()

    def finish(row, carry):
        store(row).wait()
        return carry

    lax.fori_loop(0, rows, finish, 0)


def local(
    n_su, n_sv,
    primitive, adjoint_state, objective_grad, front_height,
    shock_state, state_by_height, state_by_slope, fitted_flags,
):
    _, rows, cols, depth = primitive.shape
    f32 = jnp.float32
    vmem = pl.BlockSpec(memory_space=pltpu.VMEM)
    hbm = pl.BlockSpec(memory_space=pl.ANY)
    block = (5, rows, cols, depth)
    wide = cols + 2 * SUB
    dma = pltpu.SemaphoreType.DMA
    return pl.pallas_call(
        functools.partial(kernel, n_su, n_sv),
        out_shape=(
            jax.ShapeDtypeStruct(block, f32),
            jax.ShapeDtypeStruct((rows, cols), f32),
        ),
        in_specs=[vmem] * 5 + [hbm] * 3,
        out_specs=(hbm, vmem),
        scratch_shapes=[
            pltpu.VMEM((5, rows + 4, wide, depth), f32),
            pltpu.VMEM(block, f32),
            pltpu.VMEM(block, f32),
            pltpu.VMEM(block, f32),
            pltpu.VMEM((rows, cols, depth), f32),
            pltpu.VMEM((rows + 4, cols, depth), f32),
            pltpu.VMEM((rows, wide, depth), f32),
            pltpu.VMEM((2, 6, rows, 2, depth), f32),
            pltpu.VMEM((2, 6, rows, 2, depth), f32),
            pltpu.VMEM((cols, LANES), f32),
            pltpu.VMEM((cols, LANES), f32),
            pltpu.VMEM((cols, LANES), f32),
            pltpu.VMEM((LANES, LANES), f32),
            pltpu.VMEM((cols, LANES), f32),
            pltpu.VMEM((cols, LANES), f32),
            pltpu.VMEM((2, rows, LANES), f32),
            pltpu.VMEM((2, rows, LANES), f32),
            pltpu.VMEM((1, LANES), f32),
            pltpu.VMEM((n_su, 1, LANES), f32),
            dma((3,)),
            dma((rows,)),
            dma((8,)),
            dma((8,)),
            dma((n_su,)),
            dma((n_su,)),
        ],
        compiler_params=pltpu.CompilerParams(
            collective_id=0, has_side_effects=True, vmem_limit_bytes=40 * 1024 * 1024
        ),
    )(
        front_height, shock_state, state_by_height, state_by_slope, fitted_flags,
        primitive, adjoint_state, objective_grad,
    )


def solution(mesh):
    assert mesh.shape["nrm"] == 2
    surface = P(None, "su", "sv")
    volume = P(None, "su", "sv", "nrm")
    return jax.shard_map(
        functools.partial(local, mesh.shape["su"], mesh.shape["sv"]),
        mesh=mesh,
        in_specs=(volume,) * 3 + (P("su", "sv"),) + (surface,) * 3 + (P("su", "sv"),),
        out_specs=(volume, P("su", "sv")),
        check_vma=False,
    )
```

```python
import functools
import math

import jax
import jax.numpy as jnp
from jax import lax
from jax.experimental import pallas as pl
from jax.experimental.pallas import tpu as pltpu
from jax.sharding import PartitionSpec as P

gamma_ratio = 1.4
gamma_less = gamma_ratio - 1.0
damping_coef = 0.0625
stretch_rate = 2.2
MESH = pl.DeviceIdType.MESH
SUB = 8
LANES = 128


def thermo(state):
    speed_square = state[1] * state[1] + state[2] * state[2] + state[3] * state[3]
    kinetic = 0.5 * gamma_less * speed_square
    enthalpy = gamma_ratio * state[4] / (gamma_less * state[0]) + 0.5 * speed_square
    return (kinetic, enthalpy)


def line_flux(state, enthalpy):
    mass_flow = state[0] * state[3]
    return [
        mass_flow,
        mass_flow * state[1],
        mass_flow * state[2],
        mass_flow * state[3] + state[4],
        mass_flow * enthalpy,
    ]


def flux_transpose_normal(state, kinetic, enthalpy, adjoint):
    normal_speed = state[3]
    projected = adjoint[3]
    dotted = state[1] * adjoint[1] + state[2] * adjoint[2] + state[3] * adjoint[3]
    energy_term = adjoint[4]
    mass_row = (
        kinetic * projected
        - normal_speed * dotted
        + normal_speed * (kinetic - enthalpy) * energy_term
    )
    common = adjoint[0] + dotted + enthalpy * energy_term
    shared = projected + normal_speed * energy_term
    pieces = [mass_row]
    for component in (1, 2, 3):
        entry = normal_speed * adjoint[component] - gamma_less * state[component] * shared
        if component == 3:
            entry = entry + common
        pieces.append(entry)
    pieces.append(gamma_less * projected + gamma_ratio * normal_speed * energy_term)
    return pieces


def kernel(
    n_su, n_sv,
    height_hbm, shock_hbm, by_height_hbm, by_slope_hbm, fitted_hbm,
    prim_hbm, psi_hbm, obj_hbm,
    out, prim, enth, slope_ref, slope_t,
    psi, normal, rad_u, rad_v,
    height_ref, shock_ref, by_height_ref, by_slope_ref, fitted_ref,
    sv_send, sv_recv, edge_send, edge_recv, top_pack, turn, height_t, height_wide,
    half_send, half_recv, tot_send, tot_recv,
    load_sem, send_sem, recv_sem, tot_ssem, tot_rsem,
):
    rows, cols = prim.shape[1], prim.shape[2]
    chunks = cols // SUB
    su, sv, nrm = lax.axis_index("su"), lax.axis_index("sv"), lax.axis_index("nrm")
    own = pl.ds(SUB, cols)

    load_psi = pltpu.make_async_copy(psi_hbm, psi.at[:, pl.ds(2, rows), own], load_sem.at[0])
    load_prim = pltpu.make_async_copy(prim_hbm, prim, load_sem.at[1])
    load_obj = pltpu.make_async_copy(obj_hbm, out, load_sem.at[2])
    load_height = pltpu.make_async_copy(height_hbm, height_ref, load_sem.at[3])
    load_small = [
        pltpu.make_async_copy(shock_hbm, shock_ref, load_sem.at[4]),
        pltpu.make_async_copy(by_height_hbm, by_height_ref, load_sem.at[5]),
        pltpu.make_async_copy(by_slope_hbm, by_slope_ref, load_sem.at[6]),
        pltpu.make_async_copy(fitted_hbm, fitted_ref, load_sem.at[7]),
    ]
    load_height.start()
    load_psi.start()
    load_prim.start()

    barrier = pltpu.get_barrier_semaphore()
    for step in range(1, n_su):
        pl.semaphore_signal(
            barrier, inc=1, device_id={"su": lax.rem(su + step, n_su)}, device_id_type=MESH
        )
    pl.semaphore_signal(barrier, inc=1, device_id={"nrm": 1 - nrm}, device_id_type=MESH)

    @pl.when(sv > 0)
    def _():
        pl.semaphore_signal(barrier, inc=1, device_id={"sv": sv - 1}, device_id_type=MESH)

    @pl.when(sv < n_sv - 1)
    def _():
        pl.semaphore_signal(barrier, inc=1, device_id={"sv": sv + 1}, device_id_type=MESH)

    def remote(src, dst, slot, where):
        return pltpu.make_async_remote_copy(
            src_ref=src,
            dst_ref=dst,
            send_sem=send_sem.at[slot],
            recv_sem=recv_sem.at[slot],
            device_id=where,
            device_id_type=MESH,
        )

    psi_down = remote(
        psi_hbm.at[:, pl.ds(0, 2)], psi.at[:, pl.ds(rows + 2, 2), own], 0, {"su": su - 1}
    )
    psi_up = remote(
        psi_hbm.at[:, pl.ds(rows - 2, 2)], psi.at[:, pl.ds(0, 2), own], 1, {"su": su + 1}
    )
    rad_down = remote(rad_u.at[pl.ds(2, 2)], rad_u.at[pl.ds(rows + 2, 2)], 2, {"su": su - 1})
    rad_up = remote(rad_u.at[pl.ds(rows, 2)], rad_u.at[pl.ds(0, 2)], 3, {"su": su + 1})
    sv_down = remote(sv_send.at[0], sv_recv.at[1], 4, {"sv": sv - 1})
    sv_up = remote(sv_send.at[1], sv_recv.at[0], 5, {"sv": sv + 1})
    edge = remote(edge_send, edge_recv, 6, {"nrm": 1 - nrm})
    half = remote(half_send, half_recv, 7, {"nrm": 1 - nrm})

    for load in load_small:
        load.start()
    load_obj.start()

    lane = lax.broadcasted_iota(jnp.int32, (1, LANES), 1)
    total_depth = 2 * LANES
    place = (nrm * LANES + lane).astype(jnp.float32)
    fraction = (place + 0.5) / total_depth

    def half_inverse(position):
        return 0.5 * jnp.exp(stretch_rate * (1.0 - (position + 0.5) / total_depth))

    below = jnp.where(lane == 0, 0.0, half_inverse(place - 1.0))
    above = jnp.where(lane == LANES - 1, 0.0, half_inverse(place + 1.0))
    target = jnp.where(nrm == 0, LANES - 1, 0)
    edge_weight = jnp.where(
        lane == target,
        jnp.where(nrm == 0, -half_inverse(place + 1.0), half_inverse(place - 1.0)),
        0.0,
    )

    load_height.wait()
    turn[...] = jnp.zeros_like(turn)
    turn[0:rows, 0:cols] = 1.0 / height_ref[...]
    height_t[...] = turn[...].T[0:cols]

    def widen(row, carry):
        column = pltpu.roll(height_t[...], LANES - row, 1)[:, 0:1]
        height_wide[row] = jnp.broadcast_to(column, (cols, LANES))
        return carry

    lax.fori_loop(0, rows, widen, 0, unroll=4)

    @pl.when(su == 0)
    def _():
        psi[:, 0:2, SUB : SUB + cols] = jnp.zeros((5, 2, cols, LANES), jnp.float32)
        rad_u[0:2] = jnp.zeros((2, cols, LANES), jnp.float32)

    @pl.when(su == n_su - 1)
    def _():
        psi[:, rows + 2 : rows + 4, SUB : SUB + cols] = jnp.zeros((5, 2, cols, LANES), jnp.float32)
        rad_u[rows + 2 : rows + 4] = jnp.zeros((2, cols, LANES), jnp.float32)

    @pl.when(sv == 0)
    def _():
        sv_recv[0] = jnp.zeros((6, rows, 2, LANES), jnp.float32)

    @pl.when(sv == n_sv - 1)
    def _():
        sv_recv[1] = jnp.zeros((6, rows, 2, LANES), jnp.float32)

    neighbours = n_su + (sv > 0).astype(jnp.int32) + (sv < n_sv - 1).astype(jnp.int32)
    pl.semaphore_wait(barrier, neighbours)

    @pl.when(su > 0)
    def _():
        psi_down.start()

    @pl.when(su < n_su - 1)
    def _():
        psi_up.start()

    load_psi.wait()

    def pack(row, carry):
        top, bottom = carry
        for comp in range(5):
            spot = comp * rows + row
            rolled = pltpu.roll(psi[comp, row + 2, SUB : SUB + cols, :], spot + 1, 1)
            top = jnp.where(lane == spot, rolled, top)
            bottom = jnp.where(lane == spot + 1, rolled, bottom)
        return (top, bottom)

    blank = jnp.zeros((cols, LANES), jnp.float32)
    top, bottom = lax.fori_loop(0, rows, pack, (blank, blank), unroll=4)
    top_pack[...] = top
    edge_send[...] = jnp.where(nrm == 0, top, pltpu.roll(bottom, LANES - 1, 1))
    edge.start()

    load_prim.wait()

    def radii(row, carry):
        for chunk in range(chunks):
            part = slice(chunk * SUB, chunk * SUB + SUB)
            state = [prim[comp, row, part, :] for comp in range(5)]
            square = gamma_ratio * state[4] / state[0]
            sound = jnp.sqrt(square)
            speed_square = state[1] * state[1] + state[2] * state[2] + state[3] * state[3]
            enth[row, part, :] = square * (1.0 / gamma_less) + 0.5 * speed_square
            rad_u[row + 2, part, :] = damping_coef * (jnp.abs(state[1]) + sound)
            rad_v[row, SUB + chunk * SUB : 2 * SUB + chunk * SUB, :] = damping_coef * (
                jnp.abs(state[2]) + sound
            )
        for comp in range(5):
            sv_send[0, comp, row] = psi[comp, row + 2, SUB : SUB + 2, :]
            sv_send[1, comp, row] = psi[comp, row + 2, SUB + cols - 2 : SUB + cols, :]
        sv_send[0, 5, row] = rad_v[row, SUB : SUB + 2, :]
        sv_send[1, 5, row] = rad_v[row, SUB + cols - 2 : SUB + cols, :]
        return carry

    lax.fori_loop(0, rows, radii, 0, unroll=2)

    @pl.when(sv > 0)
    def _():
        sv_down.start()

    @pl.when(sv < n_sv - 1)
    def _():
        sv_up.start()

    @pl.when(su > 0)
    def _():
        rad_down.start()

    @pl.when(su < n_su - 1)
    def _():
        rad_up.start()

    edge.wait_recv()

    def metric_row(row, sums):
        pieces = []
        for chunk in range(chunks):
            part = slice(chunk * SUB, chunk * SUB + SUB)
            state = [prim[comp, row, part, :] for comp in range(5)]
            flux = line_flux(state, enth[row, part, :])
            factor = height_wide[row, part, :]
            total = None
            for comp in range(5):
                value = psi[comp, row + 2, SUB + chunk * SUB : 2 * SUB + chunk * SUB, :]
                shift = lax.rem(target - (comp * rows + row) + LANES, LANES)
                difference = (
                    pltpu.roll(value, 1, 1) * below
                    - pltpu.roll(value, LANES - 1, 1) * above
                    + pltpu.roll(edge_recv[part, :], shift, 1) * edge_weight
                ) * factor
                normal[comp, row, part, :] = difference
                term = flux[comp] * difference
                total = term if total is None else total + term
            pieces.append(jnp.sum(total, axis=1, keepdims=True))
        return jnp.where(lane == row, jnp.concatenate(pieces, 0), sums)

    sums = lax.fori_loop(0, rows, metric_row, blank, unroll=4)

    for load in load_small:
        load.wait()
    turn[...] = jnp.zeros_like(turn)
    turn[0:cols, :] = sums
    line_sums = turn[...].T[0:rows, 0:cols]
    turn[0:cols, :] = top_pack[...]
    tops = turn[...].T
    inverse = 1.0 / height_ref[...]
    last = 0.5 * math.exp(stretch_rate * 0.5 / total_depth)
    top_scaled = [
        tops[comp * rows : comp * rows + rows, 0:cols] * (last * inverse) for comp in range(5)
    ]
    shock = [shock_ref[comp] for comp in range(5)]
    shock_kinetic, shock_enthalpy = thermo(shock)
    shock_flux = line_flux(shock, shock_enthalpy)
    shock_adjoint = flux_transpose_normal(shock, shock_kinetic, shock_enthalpy, top_scaled)
    fitted = fitted_ref[...].astype(jnp.float32)
    front_flux = sum(top_scaled[comp] * shock_flux[comp] for comp in range(5))
    front_height = fitted * sum(shock_adjoint[comp] * by_height_ref[comp] for comp in range(5))
    front_slope = fitted * sum(shock_adjoint[comp] * by_slope_ref[comp] for comp in range(5))
    on_front = nrm == 1
    half_send[...] = jnp.zeros_like(half_send)
    half_send[0, :, 0:cols] = (
        jnp.where(on_front, front_height - front_flux * inverse, 0.0) - line_sums * inverse
    )
    half_send[1, :, 0:cols] = jnp.where(on_front, front_slope, 0.0)
    half.start()

    @pl.when(sv > 0)
    def _():
        sv_up.wait_recv()

    @pl.when(sv < n_sv - 1)
    def _():
        sv_down.wait_recv()

    def unpack(row, carry):
        for comp in range(5):
            psi[comp, row + 2, SUB - 2 : SUB, :] = sv_recv[0, comp, row]
            psi[comp, row + 2, SUB + cols : SUB + cols + 2, :] = sv_recv[1, comp, row]
        rad_v[row, SUB - 2 : SUB, :] = sv_recv[0, 5, row]
        rad_v[row, SUB + cols : SUB + cols + 2, :] = sv_recv[1, 5, row]
        return carry

    lax.fori_loop(0, rows, unpack, 0, unroll=4)
    load_obj.wait()

    def residual_row(row, carry):
        for chunk in range(chunks):
            first = chunk * SUB
            part = slice(first, first + SUB)
            wide = slice(SUB + first, 2 * SUB + first)
            density, u1, u2, u3, pressure = [prim[comp, row, part, :] for comp in range(5)]
            enthalpy = enth[row, part, :]
            ru = [rad_u[row + offset, part, :] for offset in range(5)]
            rv = [rad_v[row, wide.start + offset - 2 : wide.stop + offset - 2, :] for offset in range(5)]
            ruv = 6.0 * (ru[2] + rv[2])
            g1, g2, damped = [], [], []
            for comp in range(5):
                centre = psi[comp, row + 2, wide, :]
                along = [psi[comp, row + offset, wide, :] for offset in (0, 1, 3, 4)]
                across = [
                    psi[comp, row + 2, wide.start + offset : wide.stop + offset, :]
                    for offset in (-2, -1, 1, 2)
                ]
                g1.append((along[1] - along[2]) * (2.0 / 3.0) - (along[0] - along[3]) * (1.0 / 12.0))
                g2.append((across[1] - across[2]) * (2.0 / 3.0) - (across[0] - across[3]) * (1.0 / 12.0))
                far = ru[0] * along[0] + ru[4] * along[3] + rv[0] * across[0] + rv[4] * across[3]
                near = ru[1] * along[1] + ru[3] * along[2] + rv[1] * across[1] + rv[3] * across[2]
                damped.append(far - 4.0 * near + ruv * centre)
            g3 = [normal[comp, row, part, :] for comp in range(5)]
            kinetic = (0.5 * gamma_less) * (u1 * u1 + u2 * u2 + u3 * u3)
            speeds = (u1, u2, u3)
            grads = (g1, g2, g3)
            spread = g1[1] + g2[2] + g3[3]
            energy = u1 * g1[4] + u2 * g2[4] + u3 * g3[4]
            carried = [u1 * g1[b] + u2 * g2[b] + u3 * g3[b] for b in (1, 2, 3)]
            shared = gamma_less * (spread + energy)
            out[0, row, part, :] = (
                out[0, row, part, :]
                + damped[0]
                + kinetic * spread
                - (u1 * carried[0] + u2 * carried[1] + u3 * carried[2])
                + (kinetic - enthalpy) * energy
            )
            for b in (1, 2, 3):
                g = grads[b - 1]
                dotted = u1 * g[1] + u2 * g[2] + u3 * g[3]
                out[b, row, part, :] = (
                    out[b, row, part, :]
                    + damped[b]
                    + carried[b - 1]
                    - speeds[b - 1] * shared
                    + (g[0] + dotted + enthalpy * g[4])
                )
            out[4, row, part, :] = (
                out[4, row, part, :] + damped[4] + gamma_less * spread + gamma_ratio * energy
            )
        return carry

    middle = rows // 2
    lax.fori_loop(2, middle, residual_row, 0)

    half.wait_recv()
    summed = half_send[0, :, 0:cols] + half_recv[0, :, 0:cols]
    front_slope = half_send[1, :, 0:cols] + half_recv[1, :, 0:cols]
    step = 1
    while step < rows:
        summed = summed + jnp.concatenate(
            [summed[step:], jnp.zeros((step, cols), jnp.float32)], 0
        )
        step *= 2
    tot_send[...] = jnp.zeros_like(tot_send)
    tot_send[:, 0:cols] = summed[0:1]

    def total_copy(source, dest):
        return pltpu.make_async_remote_copy(
            src_ref=tot_send,
            dst_ref=tot_recv.at[source],
            send_sem=tot_ssem.at[dest],
            recv_sem=tot_rsem.at[source],
            device_id={"su": dest},
            device_id_type=MESH,
        )

    for other in range(n_su - 1):
        @pl.when(other < su)
        def _(other=other):
            total_copy(su, other).start()

    lax.fori_loop(middle, rows - 2, residual_row, 0)

    @pl.when(su > 0)
    def _():
        psi_up.wait_recv()
        rad_up.wait_recv()

    @pl.when(su < n_su - 1)
    def _():
        psi_down.wait_recv()
        rad_down.wait_recv()

    lax.fori_loop(0, 2, residual_row, 0)
    lax.fori_loop(rows - 2, rows, residual_row, 0)

    for other in range(1, n_su):
        @pl.when(other > su)
        def _(other=other):
            total_copy(other, su).wait_recv()

    upstream = jnp.zeros((1, cols), jnp.float32)
    for other in range(n_su - 1, 0, -1):
        upstream = upstream + jnp.where(other > su, tot_recv[other, :, 0:cols], 0.0)
    slope = (summed + upstream) * (1.0 / (rows * n_su)) + front_slope
    slope_ref[...] = slope
    turn[...] = jnp.zeros_like(turn)
    turn[0:rows, 0:cols] = slope
    slope_t[...] = turn[...].T[0:cols]

    @pl.when(su > 0)
    def _():
        psi_down.wait_send()
        rad_down.wait_send()

    @pl.when(su < n_su - 1)
    def _():
        psi_up.wait_send()
        rad_up.wait_send()

    @pl.when(sv > 0)
    def _():
        sv_down.wait_send()

    @pl.when(sv < n_sv - 1)
    def _():
        sv_up.wait_send()

    edge.wait_send()
    half.wait_send()
    for other in range(n_su - 1):
        @pl.when(other < su)
        def _(other=other):
            total_copy(su, other).wait_send()


def finish_kernel(part_ref, prim, enth, slope_ref, slope_t, out_hbm, slope_hbm, out, sem, slope_sem):
    rows, cols = prim.shape[1], prim.shape[2]
    nrm = lax.axis_index("nrm")
    store_slope = pltpu.make_async_copy(slope_ref, slope_hbm, slope_sem)
    store_slope.start()
    lane = lax.broadcasted_iota(jnp.int32, (1, LANES), 1)
    fraction = ((nrm * LANES + lane).astype(jnp.float32) + 0.5) / (2 * LANES)
    group = 4

    def store(lap):
        where = pl.ds(lap * group, group)
        return pltpu.make_async_copy(out.at[:, where], out_hbm.at[:, where], sem.at[lap])

    for lap in range(rows // group):
        for row in range(lap * group, lap * group + group):
            column = jnp.broadcast_to(slope_t[:, row : row + 1], (cols, LANES))
            for chunk in range(cols // SUB):
                part = slice(chunk * SUB, chunk * SUB + SUB)
                state = [prim[comp, row, part, :] for comp in range(5)]
                flux = line_flux(state, enth[row, part, :])
                weight = column[part] * fraction
                for comp in range(5):
                    out[comp, row, part, :] = part_ref[comp, row, part, :] + weight * flux[comp]
        store(lap).start()
    for lap in range(rows // group):
        store(lap).wait()
    store_slope.wait()


def local(
    n_su, n_sv,
    primitive, adjoint_state, objective_grad, front_height,
    shock_state, state_by_height, state_by_slope, fitted_flags,
):
    _, rows, cols, depth = primitive.shape
    f32 = jnp.float32
    vmem = pl.BlockSpec(memory_space=pltpu.VMEM)
    block = (5, rows, cols, depth)
    wide = cols + 2 * SUB
    dma = pltpu.SemaphoreType.DMA
    operands = [
        pltpu.with_memory_space_constraint(operand, pltpu.HBM)
        for operand in (
            front_height, shock_state, state_by_height, state_by_slope, fitted_flags,
            primitive, adjoint_state, objective_grad,
        )
    ]
    small = (5, rows, cols)
    hbm = pl.BlockSpec(memory_space=pltpu.HBM)
    shape = jax.ShapeDtypeStruct
    held = pl.pallas_call(
        functools.partial(kernel, n_su, n_sv),
        out_shape=(
            shape(block, f32),
            shape(block, f32),
            shape((rows, cols, depth), f32),
            shape((rows, cols), f32),
            shape((cols, LANES), f32),
        ),
        in_specs=[hbm] * 8,
        out_specs=[vmem] * 5,
        scratch_shapes=[
            pltpu.VMEM((5, rows + 4, wide, depth), f32),
            pltpu.VMEM(block, f32),
            pltpu.VMEM((rows + 4, cols, depth), f32),
            pltpu.VMEM((rows, wide, depth), f32),
            pltpu.VMEM((rows, cols), f32),
            pltpu.VMEM(small, f32),
            pltpu.VMEM(small, f32),
            pltpu.VMEM(small, f32),
            pltpu.VMEM((rows, cols), jnp.int32),
            pltpu.VMEM((2, 6, rows, 2, depth), f32),
            pltpu.VMEM((2, 6, rows, 2, depth), f32),
            pltpu.VMEM((cols, LANES), f32),
            pltpu.VMEM((cols, LANES), f32),
            pltpu.VMEM((cols, LANES), f32),
            pltpu.VMEM((LANES, LANES), f32),
            pltpu.VMEM((cols, LANES), f32),
            pltpu.VMEM((rows, cols, LANES), f32),
            pltpu.VMEM((2, rows, LANES), f32),
            pltpu.VMEM((2, rows, LANES), f32),
            pltpu.VMEM((1, LANES), f32),
            pltpu.VMEM((n_su, 1, LANES), f32),
            dma((8,)),
            dma((8,)),
            dma((8,)),
            dma((n_su,)),
            dma((n_su,)),
        ],
        compiler_params=pltpu.CompilerParams(
            collective_id=0, has_side_effects=True, vmem_limit_bytes=24 * 1024 * 1024
        ),
    )(*operands)
    return pl.pallas_call(
        finish_kernel,
        out_shape=(shape(block, f32), shape((rows, cols), f32)),
        in_specs=[vmem] * 5,
        out_specs=(hbm, hbm),
        scratch_shapes=[pltpu.VMEM(block, f32), dma((rows // 4,)), dma],
        compiler_params=pltpu.CompilerParams(vmem_limit_bytes=16 * 1024 * 1024),
    )(*held)


def solution(mesh):
    assert mesh.shape["nrm"] == 2
    surface = P(None, "su", "sv")
    volume = P(None, "su", "sv", "nrm")
    return jax.shard_map(
        functools.partial(local, mesh.shape["su"], mesh.shape["sv"]),
        mesh=mesh,
        in_specs=(volume,) * 3 + (P("su", "sv"),) + (surface,) * 3 + (P("su", "sv"),),
        out_specs=(volume, P("su", "sv")),
        check_vma=False,
    )
```

```python
import functools
import math

import jax
import jax.numpy as jnp
from jax import lax
from jax.experimental import pallas as pl
from jax.experimental.pallas import tpu as pltpu
from jax.sharding import PartitionSpec as P

gamma_ratio = 1.4
gamma_less = gamma_ratio - 1.0
damping_coef = 0.0625
stretch_rate = 2.2
MESH = pl.DeviceIdType.MESH
SUB = 8
LANES = 128


def thermo(state):
    speed_square = state[1] * state[1] + state[2] * state[2] + state[3] * state[3]
    kinetic = 0.5 * gamma_less * speed_square
    enthalpy = gamma_ratio * state[4] / (gamma_less * state[0]) + 0.5 * speed_square
    return (kinetic, enthalpy)


def line_flux(state, enthalpy):
    mass_flow = state[0] * state[3]
    return [
        mass_flow,
        mass_flow * state[1],
        mass_flow * state[2],
        mass_flow * state[3] + state[4],
        mass_flow * enthalpy,
    ]


def flux_transpose_normal(state, kinetic, enthalpy, adjoint):
    normal_speed = state[3]
    projected = adjoint[3]
    dotted = state[1] * adjoint[1] + state[2] * adjoint[2] + state[3] * adjoint[3]
    energy_term = adjoint[4]
    mass_row = (
        kinetic * projected
        - normal_speed * dotted
        + normal_speed * (kinetic - enthalpy) * energy_term
    )
    common = adjoint[0] + dotted + enthalpy * energy_term
    shared = projected + normal_speed * energy_term
    pieces = [mass_row]
    for component in (1, 2, 3):
        entry = normal_speed * adjoint[component] - gamma_less * state[component] * shared
        if component == 3:
            entry = entry + common
        pieces.append(entry)
    pieces.append(gamma_less * projected + gamma_ratio * normal_speed * energy_term)
    return pieces


def kernel(
    n_su, n_sv,
    height_hbm, shock_hbm, by_height_hbm, by_slope_hbm, fitted_hbm,
    prim_hbm, psi_hbm, obj_hbm,
    out, prim, enth, slope_ref, slope_t,
    psi, normal, rad_u, rad_v,
    height_ref, shock_ref, by_height_ref, by_slope_ref, fitted_ref,
    sv_send, sv_recv, edge_send, edge_recv, top_pack, turn, height_t, height_wide,
    half_send, half_recv, tot_send, tot_recv,
    load_sem, send_sem, recv_sem, tot_ssem, tot_rsem,
):
    rows, cols = prim.shape[1], prim.shape[2]
    chunks = cols // SUB
    su, sv, nrm = lax.axis_index("su"), lax.axis_index("sv"), lax.axis_index("nrm")
    own = pl.ds(SUB, cols)

    load_psi = pltpu.make_async_copy(psi_hbm, psi.at[:, pl.ds(2, rows), own], load_sem.at[0])
    load_prim = pltpu.make_async_copy(prim_hbm, prim, load_sem.at[1])
    load_obj = pltpu.make_async_copy(obj_hbm, out, load_sem.at[2])
    load_height = pltpu.make_async_copy(height_hbm, height_ref, load_sem.at[3])
    load_small = [
        pltpu.make_async_copy(shock_hbm, shock_ref, load_sem.at[4]),
        pltpu.make_async_copy(by_height_hbm, by_height_ref, load_sem.at[5]),
        pltpu.make_async_copy(by_slope_hbm, by_slope_ref, load_sem.at[6]),
        pltpu.make_async_copy(fitted_hbm, fitted_ref, load_sem.at[7]),
    ]
    load_height.start()
    load_psi.start()
    load_prim.start()

    barrier = pltpu.get_barrier_semaphore()
    for other in range(1, n_su):
        @pl.when(other > su)
        def _(other=other):
            for side in range(2):
                pl.semaphore_signal(
                    barrier, inc=1, device_id={"su": other, "nrm": side}, device_id_type=MESH
                )

    @pl.when(su > 0)
    def _():
        pl.semaphore_signal(barrier, inc=1, device_id={"su": su - 1}, device_id_type=MESH)

    pl.semaphore_signal(barrier, inc=1, device_id={"nrm": 1 - nrm}, device_id_type=MESH)

    @pl.when(sv > 0)
    def _():
        pl.semaphore_signal(barrier, inc=1, device_id={"sv": sv - 1}, device_id_type=MESH)

    @pl.when(sv < n_sv - 1)
    def _():
        pl.semaphore_signal(barrier, inc=1, device_id={"sv": sv + 1}, device_id_type=MESH)

    def remote(src, dst, slot, where):
        return pltpu.make_async_remote_copy(
            src_ref=src,
            dst_ref=dst,
            send_sem=send_sem.at[slot],
            recv_sem=recv_sem.at[slot],
            device_id=where,
            device_id_type=MESH,
        )

    psi_down = remote(
        psi_hbm.at[:, pl.ds(0, 2)], psi.at[:, pl.ds(rows + 2, 2), own], 0, {"su": su - 1}
    )
    psi_up = remote(
        psi_hbm.at[:, pl.ds(rows - 2, 2)], psi.at[:, pl.ds(0, 2), own], 1, {"su": su + 1}
    )
    rad_down = remote(rad_u.at[pl.ds(2, 2)], rad_u.at[pl.ds(rows + 2, 2)], 2, {"su": su - 1})
    rad_up = remote(rad_u.at[pl.ds(rows, 2)], rad_u.at[pl.ds(0, 2)], 3, {"su": su + 1})
    sv_down = remote(sv_send.at[0], sv_recv.at[1], 4, {"sv": sv - 1})
    sv_up = remote(sv_send.at[1], sv_recv.at[0], 5, {"sv": sv + 1})
    edge = remote(edge_send, edge_recv, 6, {"nrm": 1 - nrm})
    half = remote(half_send, half_recv, 7, {"nrm": 1 - nrm})

    for load in load_small:
        load.start()
    load_obj.start()

    lane = lax.broadcasted_iota(jnp.int32, (1, LANES), 1)
    total_depth = 2 * LANES
    place = (nrm * LANES + lane).astype(jnp.float32)
    fraction = (place + 0.5) / total_depth

    def half_inverse(position):
        return 0.5 * jnp.exp(stretch_rate * (1.0 - (position + 0.5) / total_depth))

    below = jnp.where(lane == 0, 0.0, half_inverse(place - 1.0))
    above = jnp.where(lane == LANES - 1, 0.0, half_inverse(place + 1.0))
    target = jnp.where(nrm == 0, LANES - 1, 0)
    edge_weight = jnp.where(
        lane == target,
        jnp.where(nrm == 0, -half_inverse(place + 1.0), half_inverse(place - 1.0)),
        0.0,
    )

    load_height.wait()
    turn[...] = jnp.zeros_like(turn)
    turn[0:rows, 0:cols] = 1.0 / height_ref[...]
    height_t[...] = turn[...].T[0:cols]

    def widen(row, carry):
        column = pltpu.roll(height_t[...], LANES - row, 1)[:, 0:1]
        height_wide[row] = jnp.broadcast_to(column, (cols, LANES))
        return carry

    lax.fori_loop(0, rows, widen, 0, unroll=4)

    @pl.when(su == 0)
    def _():
        psi[:, 0:2, SUB : SUB + cols] = jnp.zeros((5, 2, cols, LANES), jnp.float32)
        rad_u[0:2] = jnp.zeros((2, cols, LANES), jnp.float32)

    @pl.when(su == n_su - 1)
    def _():
        psi[:, rows + 2 : rows + 4, SUB : SUB + cols] = jnp.zeros((5, 2, cols, LANES), jnp.float32)
        rad_u[rows + 2 : rows + 4] = jnp.zeros((2, cols, LANES), jnp.float32)

    @pl.when(sv == 0)
    def _():
        sv_recv[0] = jnp.zeros((6, rows, 2, LANES), jnp.float32)

    @pl.when(sv == n_sv - 1)
    def _():
        sv_recv[1] = jnp.zeros((6, rows, 2, LANES), jnp.float32)

    neighbours = (
        2 * su
        + 1
        + (su < n_su - 1).astype(jnp.int32)
        + (sv > 0).astype(jnp.int32)
        + (sv < n_sv - 1).astype(jnp.int32)
    )
    pl.semaphore_wait(barrier, neighbours)

    @pl.when(su > 0)
    def _():
        psi_down.start()

    @pl.when(su < n_su - 1)
    def _():
        psi_up.start()

    load_psi.wait()

    def pack(row, carry):
        top, bottom = carry
        for comp in range(5):
            spot = comp * rows + row
            rolled = pltpu.roll(psi[comp, row + 2, SUB : SUB + cols, :], spot + 1, 1)
            top = jnp.where(lane == spot, rolled, top)
            bottom = jnp.where(lane == spot + 1, rolled, bottom)
        return (top, bottom)

    blank = jnp.zeros((cols, LANES), jnp.float32)
    top, bottom = lax.fori_loop(0, rows, pack, (blank, blank), unroll=4)
    top_pack[...] = top
    edge_send[...] = jnp.where(nrm == 0, top, pltpu.roll(bottom, LANES - 1, 1))
    edge.start()

    load_prim.wait()

    def radii(row, carry):
        for chunk in range(chunks):
            part = slice(chunk * SUB, chunk * SUB + SUB)
            state = [prim[comp, row, part, :] for comp in range(5)]
            square = gamma_ratio * state[4] / state[0]
            sound = jnp.sqrt(square)
            speed_square = state[1] * state[1] + state[2] * state[2] + state[3] * state[3]
            enth[row, part, :] = square * (1.0 / gamma_less) + 0.5 * speed_square
            rad_u[row + 2, part, :] = damping_coef * (jnp.abs(state[1]) + sound)
            rad_v[row, SUB + chunk * SUB : 2 * SUB + chunk * SUB, :] = damping_coef * (
                jnp.abs(state[2]) + sound
            )
        for comp in range(5):
            sv_send[0, comp, row] = psi[comp, row + 2, SUB : SUB + 2, :]
            sv_send[1, comp, row] = psi[comp, row + 2, SUB + cols - 2 : SUB + cols, :]
        sv_send[0, 5, row] = rad_v[row, SUB : SUB + 2, :]
        sv_send[1, 5, row] = rad_v[row, SUB + cols - 2 : SUB + cols, :]
        return carry

    lax.fori_loop(0, rows, radii, 0, unroll=2)

    @pl.when(sv > 0)
    def _():
        sv_down.start()

    @pl.when(sv < n_sv - 1)
    def _():
        sv_up.start()

    @pl.when(su > 0)
    def _():
        rad_down.start()

    @pl.when(su < n_su - 1)
    def _():
        rad_up.start()

    for load in load_small:
        load.wait()
    turn[...] = jnp.zeros_like(turn)
    turn[0:cols, :] = top_pack[...]
    tops = turn[...].T
    inverse = 1.0 / height_ref[...]
    last = 0.5 * math.exp(stretch_rate * 0.5 / total_depth)
    top_scaled = [
        tops[comp * rows : comp * rows + rows, 0:cols] * (last * inverse) for comp in range(5)
    ]
    shock = [shock_ref[comp] for comp in range(5)]
    shock_kinetic, shock_enthalpy = thermo(shock)
    shock_flux = line_flux(shock, shock_enthalpy)
    shock_adjoint = flux_transpose_normal(shock, shock_kinetic, shock_enthalpy, top_scaled)
    fitted = fitted_ref[...].astype(jnp.float32)
    front_flux = sum(top_scaled[comp] * shock_flux[comp] for comp in range(5))
    front_height = fitted * sum(shock_adjoint[comp] * by_height_ref[comp] for comp in range(5))
    front_slope = fitted * sum(shock_adjoint[comp] * by_slope_ref[comp] for comp in range(5))
    on_front = nrm == 1
    half_send[...] = jnp.zeros_like(half_send)
    half_send[0, :, 0:cols] = jnp.where(on_front, front_height - front_flux * inverse, 0.0)
    half_send[1, :, 0:cols] = jnp.where(on_front, front_slope, 0.0)
    tot_send[...] = jnp.zeros_like(tot_send)

    edge.wait_recv()

    def metric_row(row, sums):
        pieces = []
        for chunk in range(chunks):
            part = slice(chunk * SUB, chunk * SUB + SUB)
            state = [prim[comp, row, part, :] for comp in range(5)]
            flux = line_flux(state, enth[row, part, :])
            factor = height_wide[row, part, :]
            total = None
            for comp in range(5):
                value = psi[comp, row + 2, SUB + chunk * SUB : 2 * SUB + chunk * SUB, :]
                shift = lax.rem(target - (comp * rows + row) + LANES, LANES)
                difference = (
                    pltpu.roll(value, 1, 1) * below
                    - pltpu.roll(value, LANES - 1, 1) * above
                    + pltpu.roll(edge_recv[part, :], shift, 1) * edge_weight
                ) * factor
                normal[comp, row, part, :] = difference
                term = flux[comp] * difference
                total = term if total is None else total + term
            pieces.append(jnp.sum(total, axis=1, keepdims=True))
        return jnp.where(lane == row, jnp.concatenate(pieces, 0), sums)

    sums = lax.fori_loop(0, rows, metric_row, blank, unroll=4)

    turn[...] = jnp.zeros_like(turn)
    turn[0:cols, :] = sums
    part_height = half_send[0, :, 0:cols] - turn[...].T[0:rows, 0:cols] / height_ref[...]
    tot_send[:, 0:cols] = jnp.sum(part_height, axis=0, keepdims=True)

    def total_copy(source, source_side, dest, dest_side):
        return pltpu.make_async_remote_copy(
            src_ref=tot_send,
            dst_ref=tot_recv.at[source_side * n_su + source],
            send_sem=tot_ssem.at[dest_side * n_su + dest],
            recv_sem=tot_rsem.at[source_side * n_su + source],
            device_id={"su": dest, "nrm": dest_side},
            device_id_type=MESH,
        )

    for other in range(n_su - 1):
        @pl.when(other < su)
        def _(other=other):
            for side in range(2):
                total_copy(su, nrm, other, side).start()

    half_send[0, :, 0:cols] = part_height
    half.start()

    @pl.when(sv > 0)
    def _():
        sv_up.wait_recv()

    @pl.when(sv < n_sv - 1)
    def _():
        sv_down.wait_recv()

    def unpack(row, carry):
        for comp in range(5):
            psi[comp, row + 2, SUB - 2 : SUB, :] = sv_recv[0, comp, row]
            psi[comp, row + 2, SUB + cols : SUB + cols + 2, :] = sv_recv[1, comp, row]
        rad_v[row, SUB - 2 : SUB, :] = sv_recv[0, 5, row]
        rad_v[row, SUB + cols : SUB + cols + 2, :] = sv_recv[1, 5, row]
        return carry

    lax.fori_loop(0, rows, unpack, 0, unroll=4)
    load_obj.wait()

    def residual_row(row, carry):
        for chunk in range(chunks):
            first = chunk * SUB
            part = slice(first, first + SUB)
            wide = slice(SUB + first, 2 * SUB + first)
            density, u1, u2, u3, pressure = [prim[comp, row, part, :] for comp in range(5)]
            enthalpy = enth[row, part, :]
            ru = [rad_u[row + offset, part, :] for offset in range(5)]
            rv = [rad_v[row, wide.start + offset - 2 : wide.stop + offset - 2, :] for offset in range(5)]
            ruv = 6.0 * (ru[2] + rv[2])
            g1, g2, damped = [], [], []
            for comp in range(5):
                centre = psi[comp, row + 2, wide, :]
                along = [psi[comp, row + offset, wide, :] for offset in (0, 1, 3, 4)]
                across = [
                    psi[comp, row + 2, wide.start + offset : wide.stop + offset, :]
                    for offset in (-2, -1, 1, 2)
                ]
                g1.append((along[1] - along[2]) * (2.0 / 3.0) - (along[0] - along[3]) * (1.0 / 12.0))
                g2.append((across[1] - across[2]) * (2.0 / 3.0) - (across[0] - across[3]) * (1.0 / 12.0))
                far = ru[0] * along[0] + ru[4] * along[3] + rv[0] * across[0] + rv[4] * across[3]
                near = ru[1] * along[1] + ru[3] * along[2] + rv[1] * across[1] + rv[3] * across[2]
                damped.append(far - 4.0 * near + ruv * centre)
            g3 = [normal[comp, row, part, :] for comp in range(5)]
            kinetic = (0.5 * gamma_less) * (u1 * u1 + u2 * u2 + u3 * u3)
            speeds = (u1, u2, u3)
            grads = (g1, g2, g3)
            spread = g1[1] + g2[2] + g3[3]
            energy = u1 * g1[4] + u2 * g2[4] + u3 * g3[4]
            carried = [u1 * g1[b] + u2 * g2[b] + u3 * g3[b] for b in (1, 2, 3)]
            shared = gamma_less * (spread + energy)
            out[0, row, part, :] = (
                out[0, row, part, :]
                + damped[0]
                + kinetic * spread
                - (u1 * carried[0] + u2 * carried[1] + u3 * carried[2])
                + (kinetic - enthalpy) * energy
            )
            for b in (1, 2, 3):
                g = grads[b - 1]
                dotted = u1 * g[1] + u2 * g[2] + u3 * g[3]
                out[b, row, part, :] = (
                    out[b, row, part, :]
                    + damped[b]
                    + carried[b - 1]
                    - speeds[b - 1] * shared
                    + (g[0] + dotted + enthalpy * g[4])
                )
            out[4, row, part, :] = (
                out[4, row, part, :] + damped[4] + gamma_less * spread + gamma_ratio * energy
            )
        return carry

    lax.fori_loop(2, rows - 2, residual_row, 0)

    @pl.when(su > 0)
    def _():
        psi_up.wait_recv()
        rad_up.wait_recv()

    @pl.when(su < n_su - 1)
    def _():
        psi_down.wait_recv()
        rad_down.wait_recv()

    lax.fori_loop(0, 2, residual_row, 0)
    lax.fori_loop(rows - 2, rows, residual_row, 0)

    half.wait_recv()
    summed = half_send[0, :, 0:cols] + half_recv[0, :, 0:cols]
    front_slope = half_send[1, :, 0:cols] + half_recv[1, :, 0:cols]
    step = 1
    while step < rows:
        summed = summed + jnp.concatenate(
            [summed[step:], jnp.zeros((step, cols), jnp.float32)], 0
        )
        step *= 2

    for other in range(1, n_su):
        @pl.when(other > su)
        def _(other=other):
            for side in range(2):
                total_copy(other, side, su, nrm).wait_recv()

    upstream = jnp.zeros((1, cols), jnp.float32)
    for other in range(n_su - 1, 0, -1):
        both = tot_recv[other, :, 0:cols] + tot_recv[n_su + other, :, 0:cols]
        upstream = upstream + jnp.where(other > su, both, 0.0)
    slope = (summed + upstream) * (1.0 / (rows * n_su)) + front_slope
    slope_ref[...] = slope
    turn[...] = jnp.zeros_like(turn)
    turn[0:rows, 0:cols] = slope
    slope_t[...] = turn[...].T[0:cols]

    @pl.when(su > 0)
    def _():
        psi_down.wait_send()
        rad_down.wait_send()

    @pl.when(su < n_su - 1)
    def _():
        psi_up.wait_send()
        rad_up.wait_send()

    @pl.when(sv > 0)
    def _():
        sv_down.wait_send()

    @pl.when(sv < n_sv - 1)
    def _():
        sv_up.wait_send()

    edge.wait_send()
    half.wait_send()
    for other in range(n_su - 1):
        @pl.when(other < su)
        def _(other=other):
            for side in range(2):
                total_copy(su, nrm, other, side).wait_send()


def finish_kernel(part_ref, prim, enth, slope_ref, slope_t, out_hbm, slope_hbm, out, sem, slope_sem):
    rows, cols = prim.shape[1], prim.shape[2]
    nrm = lax.axis_index("nrm")
    store_slope = pltpu.make_async_copy(slope_ref, slope_hbm, slope_sem)
    store_slope.start()
    lane = lax.broadcasted_iota(jnp.int32, (1, LANES), 1)
    fraction = ((nrm * LANES + lane).astype(jnp.float32) + 0.5) / (2 * LANES)
    group = 4

    def store(lap):
        where = pl.ds(lap * group, group)
        return pltpu.make_async_copy(out.at[:, where], out_hbm.at[:, where], sem.at[lap])

    for lap in range(rows // group):
        for row in range(lap * group, lap * group + group):
            column = jnp.broadcast_to(slope_t[:, row : row + 1], (cols, LANES))
            for chunk in range(cols // SUB):
                part = slice(chunk * SUB, chunk * SUB + SUB)
                state = [prim[comp, row, part, :] for comp in range(5)]
                flux = line_flux(state, enth[row, part, :])
                weight = column[part] * fraction
                for comp in range(5):
                    out[comp, row, part, :] = part_ref[comp, row, part, :] + weight * flux[comp]
        store(lap).start()
    for lap in range(rows // group):
        store(lap).wait()
    store_slope.wait()


def local(
    n_su, n_sv,
    primitive, adjoint_state, objective_grad, front_height,
    shock_state, state_by_height, state_by_slope, fitted_flags,
):
    _, rows, cols, depth = primitive.shape
    f32 = jnp.float32
    vmem = pl.BlockSpec(memory_space=pltpu.VMEM)
    block = (5, rows, cols, depth)
    wide = cols + 2 * SUB
    dma = pltpu.SemaphoreType.DMA
    operands = [
        pltpu.with_memory_space_constraint(operand, pltpu.HBM)
        for operand in (
            front_height, shock_state, state_by_height, state_by_slope, fitted_flags,
            primitive, adjoint_state, objective_grad,
        )
    ]
    small = (5, rows, cols)
    hbm = pl.BlockSpec(memory_space=pltpu.HBM)
    shape = jax.ShapeDtypeStruct
    held = pl.pallas_call(
        functools.partial(kernel, n_su, n_sv),
        out_shape=(
            shape(block, f32),
            shape(block, f32),
            shape((rows, cols, depth), f32),
            shape((rows, cols), f32),
            shape((cols, LANES), f32),
        ),
        in_specs=[hbm] * 8,
        out_specs=[vmem] * 5,
        scratch_shapes=[
            pltpu.VMEM((5, rows + 4, wide, depth), f32),
            pltpu.VMEM(block, f32),
            pltpu.VMEM((rows + 4, cols, depth), f32),
            pltpu.VMEM((rows, wide, depth), f32),
            pltpu.VMEM((rows, cols), f32),
            pltpu.VMEM(small, f32),
            pltpu.VMEM(small, f32),
            pltpu.VMEM(small, f32),
            pltpu.VMEM((rows, cols), jnp.int32),
            pltpu.VMEM((2, 6, rows, 2, depth), f32),
            pltpu.VMEM((2, 6, rows, 2, depth), f32),
            pltpu.VMEM((cols, LANES), f32),
            pltpu.VMEM((cols, LANES), f32),
            pltpu.VMEM((cols, LANES), f32),
            pltpu.VMEM((LANES, LANES), f32),
            pltpu.VMEM((cols, LANES), f32),
            pltpu.VMEM((rows, cols, LANES), f32),
            pltpu.VMEM((2, rows, LANES), f32),
            pltpu.VMEM((2, rows, LANES), f32),
            pltpu.VMEM((1, LANES), f32),
            pltpu.VMEM((2 * n_su, 1, LANES), f32),
            dma((8,)),
            dma((8,)),
            dma((8,)),
            dma((2 * n_su,)),
            dma((2 * n_su,)),
        ],
        compiler_params=pltpu.CompilerParams(
            collective_id=0, has_side_effects=True, vmem_limit_bytes=24 * 1024 * 1024
        ),
    )(*operands)
    return pl.pallas_call(
        finish_kernel,
        out_shape=(shape(block, f32), shape((rows, cols), f32)),
        in_specs=[vmem] * 5,
        out_specs=(hbm, hbm),
        scratch_shapes=[pltpu.VMEM(block, f32), dma((rows // 4,)), dma],
        compiler_params=pltpu.CompilerParams(vmem_limit_bytes=16 * 1024 * 1024),
    )(*held)


def solution(mesh):
    assert mesh.shape["nrm"] == 2
    surface = P(None, "su", "sv")
    volume = P(None, "su", "sv", "nrm")
    return jax.shard_map(
        functools.partial(local, mesh.shape["su"], mesh.shape["sv"]),
        mesh=mesh,
        in_specs=(volume,) * 3 + (P("su", "sv"),) + (surface,) * 3 + (P("su", "sv"),),
        out_specs=(volume, P("su", "sv")),
        check_vma=False,
    )
```

```python
import functools
import math

import jax
import jax.numpy as jnp
from jax import lax
from jax.experimental import pallas as pl
from jax.experimental.pallas import tpu as pltpu
from jax.sharding import PartitionSpec as P

gamma_ratio = 1.4
gamma_less = gamma_ratio - 1.0
damping_coef = 0.0625
stretch_rate = 2.2
MESH = pl.DeviceIdType.MESH
SUB = 8
LANES = 128


def thermo(state):
    speed_square = state[1] * state[1] + state[2] * state[2] + state[3] * state[3]
    kinetic = 0.5 * gamma_less * speed_square
    enthalpy = gamma_ratio * state[4] / (gamma_less * state[0]) + 0.5 * speed_square
    return (kinetic, enthalpy)


def line_flux(state, enthalpy):
    mass_flow = state[0] * state[3]
    return [
        mass_flow,
        mass_flow * state[1],
        mass_flow * state[2],
        mass_flow * state[3] + state[4],
        mass_flow * enthalpy,
    ]


def flux_transpose_normal(state, kinetic, enthalpy, adjoint):
    normal_speed = state[3]
    projected = adjoint[3]
    dotted = state[1] * adjoint[1] + state[2] * adjoint[2] + state[3] * adjoint[3]
    energy_term = adjoint[4]
    mass_row = (
        kinetic * projected
        - normal_speed * dotted
        + normal_speed * (kinetic - enthalpy) * energy_term
    )
    common = adjoint[0] + dotted + enthalpy * energy_term
    shared = projected + normal_speed * energy_term
    pieces = [mass_row]
    for component in (1, 2, 3):
        entry = normal_speed * adjoint[component] - gamma_less * state[component] * shared
        if component == 3:
            entry = entry + common
        pieces.append(entry)
    pieces.append(gamma_less * projected + gamma_ratio * normal_speed * energy_term)
    return pieces


def kernel(
    n_su, n_sv,
    height_hbm, shock_hbm, by_height_hbm, by_slope_hbm, fitted_hbm,
    prim_hbm, psi_hbm, obj_hbm,
    out, prim, enth, slope_ref, slope_t,
    psi, normal, rad_u, rad_v,
    height_ref, shock_ref, by_height_ref, by_slope_ref, fitted_ref,
    sv_send, sv_recv, edge_send, edge_recv, top_pack, turn, height_t, height_wide,
    half_send, half_recv, tot_send, tot_recv,
    load_sem, send_sem, recv_sem, tot_ssem, tot_rsem,
):
    rows, cols = prim.shape[1], prim.shape[2]
    chunks = cols // SUB
    su, sv, nrm = lax.axis_index("su"), lax.axis_index("sv"), lax.axis_index("nrm")
    own = pl.ds(SUB, cols)
    origin = lax.div(nrm, 2)

    load_psi, load_prim, load_obj = [], [], []
    for comp in range(5):
        load_psi.append(
            pltpu.make_async_copy(
                psi_hbm.at[comp], psi.at[comp, pl.ds(2, rows), own], load_sem.at[8 + comp]
            )
        )
        load_prim.append(
            pltpu.make_async_copy(prim_hbm.at[comp], prim.at[comp], load_sem.at[13 + comp])
        )
        load_obj.append(
            pltpu.make_async_copy(obj_hbm.at[comp], out.at[comp], load_sem.at[18 + comp])
        )
    load_height = pltpu.make_async_copy(height_hbm, height_ref, load_sem.at[3])
    load_small = [
        pltpu.make_async_copy(shock_hbm, shock_ref, load_sem.at[4]),
        pltpu.make_async_copy(by_height_hbm, by_height_ref, load_sem.at[5]),
        pltpu.make_async_copy(by_slope_hbm, by_slope_ref, load_sem.at[6]),
        pltpu.make_async_copy(fitted_hbm, fitted_ref, load_sem.at[7]),
    ]
    load_height.start()
    for load in load_psi + load_prim:
        load.start()

    barrier = pltpu.get_barrier_semaphore()
    for other in range(1, n_su):
        @pl.when(other > su)
        def _(other=other):
            for side in range(2):
                pl.semaphore_signal(
                    barrier, inc=1, device_id={"su": other, "nrm": side}, device_id_type=MESH
                )

    @pl.when(su > 0)
    def _():
        pl.semaphore_signal(barrier, inc=1, device_id={"su": su - 1}, device_id_type=MESH)

    pl.semaphore_signal(barrier, inc=1, device_id={"nrm": 1 - nrm}, device_id_type=MESH)

    @pl.when(sv > 0)
    def _():
        pl.semaphore_signal(barrier, inc=1, device_id={"sv": sv - 1}, device_id_type=MESH)

    @pl.when(sv < n_sv - 1)
    def _():
        pl.semaphore_signal(barrier, inc=1, device_id={"sv": sv + 1}, device_id_type=MESH)

    def remote(src, dst, slot, where):
        return pltpu.make_async_remote_copy(
            src_ref=src,
            dst_ref=dst,
            send_sem=send_sem.at[slot],
            recv_sem=recv_sem.at[slot],
            device_id=where,
            device_id_type=MESH,
        )

    psi_down = remote(
        psi_hbm.at[:, pl.ds(0, 2)], psi.at[:, pl.ds(rows + 2, 2), own], 0, {"su": su - 1}
    )
    psi_up = remote(
        psi_hbm.at[:, pl.ds(rows - 2, 2)], psi.at[:, pl.ds(0, 2), own], 1, {"su": su + 1}
    )
    rad_down = remote(rad_u.at[pl.ds(2, 2)], rad_u.at[pl.ds(rows + 2, 2)], 2, {"su": su - 1})
    rad_up = remote(rad_u.at[pl.ds(rows, 2)], rad_u.at[pl.ds(0, 2)], 3, {"su": su + 1})
    sv_down = remote(sv_send.at[0], sv_recv.at[1], 4, {"sv": sv - 1})
    sv_up = remote(sv_send.at[1], sv_recv.at[0], 5, {"sv": sv + 1})
    edge = remote(edge_send, edge_recv, 6, {"nrm": 1 - nrm})
    half = remote(half_send, half_recv, 7, {"nrm": 1 - nrm})

    for load in load_small + load_obj:
        load.start()

    lane = lax.broadcasted_iota(jnp.int32, (1, LANES), 1)
    total_depth = 2 * LANES
    place = (nrm * LANES + lane).astype(jnp.float32)
    fraction = (place + 0.5) / total_depth

    def half_inverse(position):
        return 0.5 * jnp.exp(stretch_rate * (1.0 - (position + 0.5) / total_depth))

    below = jnp.where(lane == 0, 0.0, half_inverse(place - 1.0))
    above = jnp.where(lane == LANES - 1, 0.0, half_inverse(place + 1.0))
    target = jnp.where(nrm == 0, LANES - 1, 0)
    edge_weight = jnp.where(
        lane == target,
        jnp.where(nrm == 0, -half_inverse(place + 1.0), half_inverse(place - 1.0)),
        0.0,
    )

    load_height.wait()
    turn[...] = jnp.zeros_like(turn)
    turn[0:rows, 0:cols] = 1.0 / height_ref[...]
    height_t[...] = turn[...].T[0:cols]

    def widen(row, carry):
        column = pltpu.roll(height_t[...], LANES - row, 1)[:, 0:1]
        height_wide[row] = jnp.broadcast_to(column, (cols, LANES))
        return carry

    lax.fori_loop(0, rows, widen, 0, unroll=4)

    @pl.when(su == 0)
    def _():
        psi[:, 0:2, SUB : SUB + cols] = jnp.zeros((5, 2, cols, LANES), jnp.float32)
        rad_u[0:2] = jnp.zeros((2, cols, LANES), jnp.float32)

    @pl.when(su == n_su - 1)
    def _():
        psi[:, rows + 2 : rows + 4, SUB : SUB + cols] = jnp.zeros((5, 2, cols, LANES), jnp.float32)
        rad_u[rows + 2 : rows + 4] = jnp.zeros((2, cols, LANES), jnp.float32)

    @pl.when(sv == 0)
    def _():
        sv_recv[0] = jnp.zeros((6, rows, 2, LANES), jnp.float32)

    @pl.when(sv == n_sv - 1)
    def _():
        sv_recv[1] = jnp.zeros((6, rows, 2, LANES), jnp.float32)

    neighbours = (
        2 * su
        + 1
        + (su < n_su - 1).astype(jnp.int32)
        + (sv > 0).astype(jnp.int32)
        + (sv < n_sv - 1).astype(jnp.int32)
    )
    pl.semaphore_wait(barrier, neighbours)

    @pl.when(su > 0)
    def _():
        psi_down.start()

    @pl.when(su < n_su - 1)
    def _():
        psi_up.start()

    for load in load_psi:
        load.wait()

    def pack(row, carry):
        top, bottom = carry
        for comp in range(5):
            spot = comp * rows + row
            rolled = pltpu.roll(psi[comp, row + 2, SUB : SUB + cols, :], spot + 1, 1)
            top = jnp.where(lane == spot, rolled, top)
            bottom = jnp.where(lane == spot + 1, rolled, bottom)
        return (top, bottom)

    blank = jnp.zeros((cols, LANES), jnp.float32)
    top, bottom = lax.fori_loop(0, rows, pack, (blank, blank), unroll=4)
    top_pack[...] = top
    edge_send[...] = jnp.where(nrm == 0, top, pltpu.roll(bottom, LANES - 1, 1))
    edge.start()

    for load in load_prim:
        load.wait()

    def radii(row, carry):
        for chunk in range(chunks):
            part = slice(chunk * SUB, chunk * SUB + SUB)
            state = [prim[comp, row, part, :] for comp in range(5)]
            square = gamma_ratio * state[4] / state[0]
            sound = jnp.sqrt(square)
            speed_square = state[1] * state[1] + state[2] * state[2] + state[3] * state[3]
            enth[row, part, :] = square * (1.0 / gamma_less) + 0.5 * speed_square
            rad_u[row + 2, part, :] = damping_coef * (jnp.abs(state[1]) + sound)
            rad_v[row, SUB + chunk * SUB : 2 * SUB + chunk * SUB, :] = damping_coef * (
                jnp.abs(state[2]) + sound
            )
        for comp in range(5):
            sv_send[0, comp, row] = psi[comp, row + 2, SUB : SUB + 2, :]
            sv_send[1, comp, row] = psi[comp, row + 2, SUB + cols - 2 : SUB + cols, :]
        sv_send[0, 5, row] = rad_v[row, SUB : SUB + 2, :]
        sv_send[1, 5, row] = rad_v[row, SUB + cols - 2 : SUB + cols, :]
        return carry

    lax.fori_loop(0, rows, radii, 0, unroll=2)

    @pl.when(sv > 0)
    def _():
        sv_down.start()

    @pl.when(sv < n_sv - 1)
    def _():
        sv_up.start()

    @pl.when(su > 0)
    def _():
        rad_down.start()

    @pl.when(su < n_su - 1)
    def _():
        rad_up.start()

    for load in load_small:
        load.wait()
    turn[...] = jnp.zeros_like(turn)
    turn[0:cols, :] = top_pack[...]
    tops = turn[...].T
    inverse = 1.0 / height_ref[...]
    last = 0.5 * math.exp(stretch_rate * 0.5 / total_depth)
    top_scaled = [
        tops[comp * rows : comp * rows + rows, 0:cols] * (last * inverse) for comp in range(5)
    ]
    shock = [shock_ref[comp] for comp in range(5)]
    shock_kinetic, shock_enthalpy = thermo(shock)
    shock_flux = line_flux(shock, shock_enthalpy)
    shock_adjoint = flux_transpose_normal(shock, shock_kinetic, shock_enthalpy, top_scaled)
    fitted = fitted_ref[...].astype(jnp.float32)
    front_flux = sum(top_scaled[comp] * shock_flux[comp] for comp in range(5))
    front_height = fitted * sum(shock_adjoint[comp] * by_height_ref[comp] for comp in range(5))
    front_slope = fitted * sum(shock_adjoint[comp] * by_slope_ref[comp] for comp in range(5))
    on_front = nrm == 1
    half_send[...] = jnp.zeros_like(half_send)
    half_send[0, :, 0:cols] = jnp.where(on_front, front_height - front_flux * inverse, 0.0)
    half_send[1, :, 0:cols] = jnp.where(on_front, front_slope, 0.0)
    tot_send[...] = jnp.zeros_like(tot_send)

    edge.wait_recv()

    def metric_row(row, sums):
        pieces = []
        for chunk in range(chunks):
            part = slice(chunk * SUB, chunk * SUB + SUB)
            state = [prim[comp, row, part, :] for comp in range(5)]
            flux = line_flux(state, enth[row, part, :])
            factor = height_wide[row, part, :]
            total = None
            for comp in range(5):
                value = psi[comp, row + 2, SUB + chunk * SUB : 2 * SUB + chunk * SUB, :]
                shift = lax.rem(target - (comp * rows + row) + LANES, LANES)
                difference = (
                    pltpu.roll(value, 1, 1) * below
                    - pltpu.roll(value, LANES - 1, 1) * above
                    + pltpu.roll(edge_recv[part, :], shift, 1) * edge_weight
                ) * factor
                normal[comp, row, part, :] = difference
                term = flux[comp] * difference
                total = term if total is None else total + term
            pieces.append(jnp.sum(total, axis=1, keepdims=True))
        return jnp.where(lane == row, jnp.concatenate(pieces, 0), sums)

    sums = lax.fori_loop(0, rows, metric_row, blank, unroll=4)

    turn[...] = jnp.zeros_like(turn)
    turn[0:cols, :] = sums
    part_height = half_send[0, :, 0:cols] - turn[...].T[0:rows, 0:cols] / height_ref[...]
    tot_send[:, 0:cols] = jnp.sum(part_height, axis=0, keepdims=True)

    half_send[0, :, 0:cols] = part_height
    half.start()

    def total_copy(source, source_side, dest, dest_side):
        return pltpu.make_async_remote_copy(
            src_ref=tot_send,
            dst_ref=tot_recv.at[source_side * n_su + source],
            send_sem=tot_ssem.at[dest_side * n_su + dest],
            recv_sem=tot_rsem.at[source_side * n_su + source],
            device_id={"su": dest, "nrm": dest_side},
            device_id_type=MESH,
        )

    for other in range(n_su - 1):
        @pl.when(other < su)
        def _(other=other):
            for side in range(2):
                total_copy(su, nrm, other, side).start()

    @pl.when(sv > 0)
    def _():
        sv_up.wait_recv()

    @pl.when(sv < n_sv - 1)
    def _():
        sv_down.wait_recv()

    def unpack(row, carry):
        for comp in range(5):
            psi[comp, row + 2, SUB - 2 : SUB, :] = sv_recv[0, comp, row]
            psi[comp, row + 2, SUB + cols : SUB + cols + 2, :] = sv_recv[1, comp, row]
        rad_v[row, SUB - 2 : SUB, :] = sv_recv[0, 5, row]
        rad_v[row, SUB + cols : SUB + cols + 2, :] = sv_recv[1, 5, row]
        return carry

    lax.fori_loop(0, rows, unpack, 0, unroll=4)
    for load in load_obj:
        load.wait()

    def residual_row(row, carry):
        for chunk in range(chunks):
            first = chunk * SUB
            part = slice(first, first + SUB)
            wide = slice(SUB + first, 2 * SUB + first)
            density, u1, u2, u3, pressure = [prim[comp, row, part, :] for comp in range(5)]
            enthalpy = enth[row, part, :]
            ru = [rad_u[row + offset, part, :] for offset in range(5)]
            rv = [
                rad_v[row, pl.ds(wide.start + offset - 2 + origin, SUB), :] for offset in range(5)
            ]
            ruv = 6.0 * (ru[2] + rv[2])
            g1, g2, damped = [], [], []
            for comp in range(5):
                centre = psi[comp, row + 2, wide, :]
                along = [psi[comp, row + offset, wide, :] for offset in (0, 1, 3, 4)]
                across = [
                    psi[comp, row + 2, pl.ds(wide.start + offset + origin, SUB), :]
                    for offset in (-2, -1, 1, 2)
                ]
                g1.append((along[1] - along[2]) * (2.0 / 3.0) - (along[0] - along[3]) * (1.0 / 12.0))
                g2.append((across[1] - across[2]) * (2.0 / 3.0) - (across[0] - across[3]) * (1.0 / 12.0))
                far = ru[0] * along[0] + ru[4] * along[3] + rv[0] * across[0] + rv[4] * across[3]
                near = ru[1] * along[1] + ru[3] * along[2] + rv[1] * across[1] + rv[3] * across[2]
                damped.append(far - 4.0 * near + ruv * centre)
            g3 = [normal[comp, row, part, :] for comp in range(5)]
            kinetic = (0.5 * gamma_less) * (u1 * u1 + u2 * u2 + u3 * u3)
            speeds = (u1, u2, u3)
            grads = (g1, g2, g3)
            spread = g1[1] + g2[2] + g3[3]
            energy = u1 * g1[4] + u2 * g2[4] + u3 * g3[4]
            carried = [u1 * g1[b] + u2 * g2[b] + u3 * g3[b] for b in (1, 2, 3)]
            shared = gamma_less * (spread + energy)
            out[0, row, part, :] = (
                out[0, row, part, :]
                + damped[0]
                + kinetic * spread
                - (u1 * carried[0] + u2 * carried[1] + u3 * carried[2])
                + (kinetic - enthalpy) * energy
            )
            for b in (1, 2, 3):
                g = grads[b - 1]
                dotted = u1 * g[1] + u2 * g[2] + u3 * g[3]
                out[b, row, part, :] = (
                    out[b, row, part, :]
                    + damped[b]
                    + carried[b - 1]
                    - speeds[b - 1] * shared
                    + (g[0] + dotted + enthalpy * g[4])
                )
            out[4, row, part, :] = (
                out[4, row, part, :] + damped[4] + gamma_less * spread + gamma_ratio * energy
            )
        return carry

    lax.fori_loop(2, rows - 2, residual_row, 0)

    @pl.when(su > 0)
    def _():
        psi_up.wait_recv()
        rad_up.wait_recv()

    @pl.when(su < n_su - 1)
    def _():
        psi_down.wait_recv()
        rad_down.wait_recv()

    lax.fori_loop(0, 2, residual_row, 0)
    lax.fori_loop(rows - 2, rows, residual_row, 0)

    half.wait_recv()
    summed = half_send[0, :, 0:cols] + half_recv[0, :, 0:cols]
    front_slope = half_send[1, :, 0:cols] + half_recv[1, :, 0:cols]
    step = 1
    while step < rows:
        summed = summed + jnp.concatenate(
            [summed[step:], jnp.zeros((step, cols), jnp.float32)], 0
        )
        step *= 2

    for other in range(1, n_su):
        @pl.when(other > su)
        def _(other=other):
            for side in range(2):
                total_copy(other, side, su, nrm).wait_recv()

    upstream = jnp.zeros((1, cols), jnp.float32)
    for other in range(n_su - 1, 0, -1):
        both = tot_recv[other, :, 0:cols] + tot_recv[n_su + other, :, 0:cols]
        upstream = upstream + jnp.where(other > su, both, 0.0)
    slope = (summed + upstream) * (1.0 / (rows * n_su)) + front_slope
    slope_ref[...] = slope
    turn[...] = jnp.zeros_like(turn)
    turn[0:rows, 0:cols] = slope
    slope_t[...] = turn[...].T[0:cols]

    @pl.when(su > 0)
    def _():
        psi_down.wait_send()
        rad_down.wait_send()

    @pl.when(su < n_su - 1)
    def _():
        psi_up.wait_send()
        rad_up.wait_send()

    @pl.when(sv > 0)
    def _():
        sv_down.wait_send()

    @pl.when(sv < n_sv - 1)
    def _():
        sv_up.wait_send()

    edge.wait_send()
    half.wait_send()
    for other in range(n_su - 1):
        @pl.when(other < su)
        def _(other=other):
            for side in range(2):
                total_copy(su, nrm, other, side).wait_send()


def finish_kernel(part_ref, prim, enth, slope_ref, slope_t, out_hbm, slope_hbm, out, sem, slope_sem):
    rows, cols = prim.shape[1], prim.shape[2]
    nrm = lax.axis_index("nrm")
    store_slope = pltpu.make_async_copy(slope_ref, slope_hbm, slope_sem)
    store_slope.start()
    lane = lax.broadcasted_iota(jnp.int32, (1, LANES), 1)
    fraction = ((nrm * LANES + lane).astype(jnp.float32) + 0.5) / (2 * LANES)
    group = 4

    def store(lap):
        where = pl.ds(lap * group, group)
        return pltpu.make_async_copy(out.at[:, where], out_hbm.at[:, where], sem.at[lap])

    for lap in range(rows // group):
        for row in range(lap * group, lap * group + group):
            column = jnp.broadcast_to(slope_t[:, row : row + 1], (cols, LANES))
            for chunk in range(cols // SUB):
                part = slice(chunk * SUB, chunk * SUB + SUB)
                state = [prim[comp, row, part, :] for comp in range(5)]
                flux = line_flux(state, enth[row, part, :])
                weight = column[part] * fraction
                for comp in range(5):
                    out[comp, row, part, :] = part_ref[comp, row, part, :] + weight * flux[comp]
        store(lap).start()
    for lap in range(rows // group):
        store(lap).wait()
    store_slope.wait()


def local(
    n_su, n_sv,
    primitive, adjoint_state, objective_grad, front_height,
    shock_state, state_by_height, state_by_slope, fitted_flags,
):
    _, rows, cols, depth = primitive.shape
    f32 = jnp.float32
    vmem = pl.BlockSpec(memory_space=pltpu.VMEM)
    block = (5, rows, cols, depth)
    wide = cols + 2 * SUB
    dma = pltpu.SemaphoreType.DMA
    operands = [
        pltpu.with_memory_space_constraint(operand, pltpu.HBM)
        for operand in (
            front_height, shock_state, state_by_height, state_by_slope, fitted_flags,
            primitive, adjoint_state, objective_grad,
        )
    ]
    small = (5, rows, cols)
    hbm = pl.BlockSpec(memory_space=pltpu.HBM)
    shape = jax.ShapeDtypeStruct
    held = pl.pallas_call(
        functools.partial(kernel, n_su, n_sv),
        out_shape=(
            shape(block, f32),
            shape(block, f32),
            shape((rows, cols, depth), f32),
            shape((rows, cols), f32),
            shape((cols, LANES), f32),
        ),
        in_specs=[hbm] * 8,
        out_specs=[vmem] * 5,
        scratch_shapes=[
            pltpu.VMEM((5, rows + 4, wide, depth), f32),
            pltpu.VMEM(block, f32),
            pltpu.VMEM((rows + 4, cols, depth), f32),
            pltpu.VMEM((rows, wide, depth), f32),
            pltpu.VMEM((rows, cols), f32),
            pltpu.VMEM(small, f32),
            pltpu.VMEM(small, f32),
            pltpu.VMEM(small, f32),
            pltpu.VMEM((rows, cols), jnp.int32),
            pltpu.VMEM((2, 6, rows, 2, depth), f32),
            pltpu.VMEM((2, 6, rows, 2, depth), f32),
            pltpu.VMEM((cols, LANES), f32),
            pltpu.VMEM((cols, LANES), f32),
            pltpu.VMEM((cols, LANES), f32),
            pltpu.VMEM((LANES, LANES), f32),
            pltpu.VMEM((cols, LANES), f32),
            pltpu.VMEM((rows, cols, LANES), f32),
            pltpu.VMEM((2, rows, LANES), f32),
            pltpu.VMEM((2, rows, LANES), f32),
            pltpu.VMEM((1, LANES), f32),
            pltpu.VMEM((2 * n_su, 1, LANES), f32),
            dma((23,)),
            dma((8,)),
            dma((8,)),
            dma((2 * n_su,)),
            dma((2 * n_su,)),
        ],
        compiler_params=pltpu.CompilerParams(
            collective_id=0, has_side_effects=True, vmem_limit_bytes=24 * 1024 * 1024
        ),
    )(*operands)
    return pl.pallas_call(
        finish_kernel,
        out_shape=(shape(block, f32), shape((rows, cols), f32)),
        in_specs=[vmem] * 5,
        out_specs=(hbm, hbm),
        scratch_shapes=[pltpu.VMEM(block, f32), dma((rows // 4,)), dma],
        compiler_params=pltpu.CompilerParams(vmem_limit_bytes=16 * 1024 * 1024),
    )(*held)


def solution(mesh):
    assert mesh.shape["nrm"] == 2
    surface = P(None, "su", "sv")
    volume = P(None, "su", "sv", "nrm")
    return jax.shard_map(
        functools.partial(local, mesh.shape["su"], mesh.shape["sv"]),
        mesh=mesh,
        in_specs=(volume,) * 3 + (P("su", "sv"),) + (surface,) * 3 + (P("su", "sv"),),
        out_specs=(volume, P("su", "sv")),
        check_vma=False,
    )
```

```python
import functools
import math

import jax
import jax.numpy as jnp
from jax import lax
from jax.experimental import pallas as pl
from jax.experimental.pallas import tpu as pltpu
from jax.sharding import PartitionSpec as P

gamma_ratio = 1.4
gamma_less = gamma_ratio - 1.0
damping_coef = 0.0625
stretch_rate = 2.2
MESH = pl.DeviceIdType.MESH
SUB = 8
LANES = 128


def thermo(state):
    speed_square = state[1] * state[1] + state[2] * state[2] + state[3] * state[3]
    kinetic = 0.5 * gamma_less * speed_square
    enthalpy = gamma_ratio * state[4] / (gamma_less * state[0]) + 0.5 * speed_square
    return (kinetic, enthalpy)


def line_flux(state, enthalpy):
    mass_flow = state[0] * state[3]
    return [
        mass_flow,
        mass_flow * state[1],
        mass_flow * state[2],
        mass_flow * state[3] + state[4],
        mass_flow * enthalpy,
    ]


def flux_transpose_normal(state, kinetic, enthalpy, adjoint):
    normal_speed = state[3]
    projected = adjoint[3]
    dotted = state[1] * adjoint[1] + state[2] * adjoint[2] + state[3] * adjoint[3]
    energy_term = adjoint[4]
    mass_row = (
        kinetic * projected
        - normal_speed * dotted
        + normal_speed * (kinetic - enthalpy) * energy_term
    )
    common = adjoint[0] + dotted + enthalpy * energy_term
    shared = projected + normal_speed * energy_term
    pieces = [mass_row]
    for component in (1, 2, 3):
        entry = normal_speed * adjoint[component] - gamma_less * state[component] * shared
        if component == 3:
            entry = entry + common
        pieces.append(entry)
    pieces.append(gamma_less * projected + gamma_ratio * normal_speed * energy_term)
    return pieces


def kernel(
    n_su, n_sv,
    height_hbm, shock_hbm, by_height_hbm, by_slope_hbm, fitted_hbm,
    prim_hbm, psi_hbm, obj_hbm,
    out, prim, enth, slope_ref, slope_t,
    psi, normal, rad_u, rad_v,
    height_ref, shock_ref, by_height_ref, by_slope_ref, fitted_ref,
    sv_send, sv_recv, edge_send, edge_recv, top_pack, turn, height_t, height_wide, band, line_terms,
    half_send, half_recv, tot_send, tot_recv,
    load_sem, send_sem, recv_sem, tot_ssem, tot_rsem,
):
    rows, cols = prim.shape[1], prim.shape[2]
    chunks = cols // SUB
    su, sv, nrm = lax.axis_index("su"), lax.axis_index("sv"), lax.axis_index("nrm")
    own = pl.ds(SUB, cols)

    load_psi = pltpu.make_async_copy(psi_hbm, psi.at[:, pl.ds(2, rows), own], load_sem.at[0])
    load_prim = pltpu.make_async_copy(prim_hbm, prim, load_sem.at[1])
    load_obj = pltpu.make_async_copy(obj_hbm, out, load_sem.at[2])
    load_height = pltpu.make_async_copy(height_hbm, height_ref, load_sem.at[3])
    load_small = [
        pltpu.make_async_copy(shock_hbm, shock_ref, load_sem.at[4]),
        pltpu.make_async_copy(by_height_hbm, by_height_ref, load_sem.at[5]),
        pltpu.make_async_copy(by_slope_hbm, by_slope_ref, load_sem.at[6]),
        pltpu.make_async_copy(fitted_hbm, fitted_ref, load_sem.at[7]),
    ]
    load_height.start()
    load_psi.start()
    load_prim.start()

    barrier = pltpu.get_barrier_semaphore()
    for other in range(1, n_su):
        @pl.when(other > su)
        def _(other=other):
            for side in range(2):
                pl.semaphore_signal(
                    barrier, inc=1, device_id={"su": other, "nrm": side}, device_id_type=MESH
                )

    @pl.when(su > 0)
    def _():
        pl.semaphore_signal(barrier, inc=1, device_id={"su": su - 1}, device_id_type=MESH)

    pl.semaphore_signal(barrier, inc=1, device_id={"nrm": 1 - nrm}, device_id_type=MESH)

    @pl.when(sv > 0)
    def _():
        pl.semaphore_signal(barrier, inc=1, device_id={"sv": sv - 1}, device_id_type=MESH)

    @pl.when(sv < n_sv - 1)
    def _():
        pl.semaphore_signal(barrier, inc=1, device_id={"sv": sv + 1}, device_id_type=MESH)

    def remote(src, dst, slot, where):
        return pltpu.make_async_remote_copy(
            src_ref=src,
            dst_ref=dst,
            send_sem=send_sem.at[slot],
            recv_sem=recv_sem.at[slot],
            device_id=where,
            device_id_type=MESH,
        )

    psi_down = remote(
        psi_hbm.at[:, pl.ds(0, 2)], psi.at[:, pl.ds(rows + 2, 2), own], 0, {"su": su - 1}
    )
    psi_up = remote(
        psi_hbm.at[:, pl.ds(rows - 2, 2)], psi.at[:, pl.ds(0, 2), own], 1, {"su": su + 1}
    )
    rad_down = remote(rad_u.at[pl.ds(2, 2)], rad_u.at[pl.ds(rows + 2, 2)], 2, {"su": su - 1})
    rad_up = remote(rad_u.at[pl.ds(rows, 2)], rad_u.at[pl.ds(0, 2)], 3, {"su": su + 1})
    sv_down = remote(sv_send.at[0], sv_recv.at[1], 4, {"sv": sv - 1})
    sv_up = remote(sv_send.at[1], sv_recv.at[0], 5, {"sv": sv + 1})
    edge = remote(edge_send, edge_recv, 6, {"nrm": 1 - nrm})
    half = remote(half_send, half_recv, 7, {"nrm": 1 - nrm})

    for load in load_small:
        load.start()
    load_obj.start()

    lane = lax.broadcasted_iota(jnp.int32, (1, LANES), 1)
    total_depth = 2 * LANES
    place = (nrm * LANES + lane).astype(jnp.float32)
    fraction = (place + 0.5) / total_depth

    def half_inverse(position):
        return 0.5 * jnp.exp(stretch_rate * (1.0 - (position + 0.5) / total_depth))

    own_weight = half_inverse(place)
    source = lax.rem(lax.broadcasted_iota(jnp.int32, (2 * LANES, LANES), 0), LANES)
    column = lax.broadcasted_iota(jnp.int32, (2 * LANES, LANES), 1)
    band[...] = (source == column - 1).astype(jnp.float32) - (source == column + 1).astype(
        jnp.float32
    )
    target = jnp.where(nrm == 0, LANES - 1, 0)
    edge_weight = jnp.where(
        lane == target,
        jnp.where(nrm == 0, -half_inverse(place + 1.0), half_inverse(place - 1.0)),
        0.0,
    )

    load_height.wait()
    turn[...] = jnp.zeros_like(turn)
    turn[0:rows, 0:cols] = 1.0 / height_ref[...]
    height_t[...] = turn[...].T[0:cols]

    def widen(row, carry):
        column = pltpu.roll(height_t[...], LANES - row, 1)[:, 0:1]
        height_wide[row] = jnp.broadcast_to(column, (cols, LANES))
        return carry

    lax.fori_loop(0, rows, widen, 0, unroll=4)

    @pl.when(su == 0)
    def _():
        psi[:, 0:2, SUB : SUB + cols] = jnp.zeros((5, 2, cols, LANES), jnp.float32)
        rad_u[0:2] = jnp.zeros((2, cols, LANES), jnp.float32)

    @pl.when(su == n_su - 1)
    def _():
        psi[:, rows + 2 : rows + 4, SUB : SUB + cols] = jnp.zeros((5, 2, cols, LANES), jnp.float32)
        rad_u[rows + 2 : rows + 4] = jnp.zeros((2, cols, LANES), jnp.float32)

    @pl.when(sv == 0)
    def _():
        sv_recv[0] = jnp.zeros((6, rows, 2, LANES), jnp.float32)

    @pl.when(sv == n_sv - 1)
    def _():
        sv_recv[1] = jnp.zeros((6, rows, 2, LANES), jnp.float32)

    neighbours = (
        2 * su
        + 1
        + (su < n_su - 1).astype(jnp.int32)
        + (sv > 0).astype(jnp.int32)
        + (sv < n_sv - 1).astype(jnp.int32)
    )
    pl.semaphore_wait(barrier, neighbours)

    @pl.when(su > 0)
    def _():
        psi_down.start()

    @pl.when(su < n_su - 1)
    def _():
        psi_up.start()

    load_psi.wait()

    def pack(row, carry):
        top, bottom = carry
        for comp in range(5):
            spot = comp * rows + row
            rolled = pltpu.roll(psi[comp, row + 2, SUB : SUB + cols, :], spot + 1, 1)
            top = jnp.where(lane == spot, rolled, top)
            bottom = jnp.where(lane == spot + 1, rolled, bottom)
        return (top, bottom)

    blank = jnp.zeros((cols, LANES), jnp.float32)
    top, bottom = lax.fori_loop(0, rows, pack, (blank, blank), unroll=4)
    top_pack[...] = top
    edge_send[...] = jnp.where(nrm == 0, top, pltpu.roll(bottom, LANES - 1, 1))
    edge.start()

    load_prim.wait()

    def radii(row, carry):
        for chunk in range(chunks):
            part = slice(chunk * SUB, chunk * SUB + SUB)
            state = [prim[comp, row, part, :] for comp in range(5)]
            square = gamma_ratio * state[4] / state[0]
            sound = jnp.sqrt(square)
            speed_square = state[1] * state[1] + state[2] * state[2] + state[3] * state[3]
            enth[row, part, :] = square * (1.0 / gamma_less) + 0.5 * speed_square
            rad_u[row + 2, part, :] = damping_coef * (jnp.abs(state[1]) + sound)
            rad_v[row, SUB + chunk * SUB : 2 * SUB + chunk * SUB, :] = damping_coef * (
                jnp.abs(state[2]) + sound
            )
        for comp in range(5):
            sv_send[0, comp, row] = psi[comp, row + 2, SUB : SUB + 2, :]
            sv_send[1, comp, row] = psi[comp, row + 2, SUB + cols - 2 : SUB + cols, :]
        sv_send[0, 5, row] = rad_v[row, SUB : SUB + 2, :]
        sv_send[1, 5, row] = rad_v[row, SUB + cols - 2 : SUB + cols, :]
        return carry

    lax.fori_loop(0, rows, radii, 0, unroll=2)

    @pl.when(sv > 0)
    def _():
        sv_down.start()

    @pl.when(sv < n_sv - 1)
    def _():
        sv_up.start()

    @pl.when(su > 0)
    def _():
        rad_down.start()

    @pl.when(su < n_su - 1)
    def _():
        rad_up.start()

    for load in load_small:
        load.wait()
    turn[...] = jnp.zeros_like(turn)
    turn[0:cols, :] = top_pack[...]
    tops = turn[...].T
    inverse = 1.0 / height_ref[...]
    last = 0.5 * math.exp(stretch_rate * 0.5 / total_depth)
    top_scaled = [
        tops[comp * rows : comp * rows + rows, 0:cols] * (last * inverse) for comp in range(5)
    ]
    shock = [shock_ref[comp] for comp in range(5)]
    shock_kinetic, shock_enthalpy = thermo(shock)
    shock_flux = line_flux(shock, shock_enthalpy)
    shock_adjoint = flux_transpose_normal(shock, shock_kinetic, shock_enthalpy, top_scaled)
    fitted = fitted_ref[...].astype(jnp.float32)
    front_flux = sum(top_scaled[comp] * shock_flux[comp] for comp in range(5))
    front_height = fitted * sum(shock_adjoint[comp] * by_height_ref[comp] for comp in range(5))
    front_slope = fitted * sum(shock_adjoint[comp] * by_slope_ref[comp] for comp in range(5))
    on_front = nrm == 1
    half_send[...] = jnp.zeros_like(half_send)
    half_send[0, :, 0:cols] = jnp.where(on_front, front_height - front_flux * inverse, 0.0)
    half_send[1, :, 0:cols] = jnp.where(on_front, front_slope, 0.0)
    tot_send[...] = jnp.zeros_like(tot_send)

    edge.wait_recv()

    group = 4

    def split(value):
        coarse = value.astype(jnp.bfloat16).astype(jnp.float32)
        return jnp.concatenate([coarse, value - coarse], 1)

    def metric_rows(lap, carry):
        first = lap * group
        lines = [
            psi[comp, first + step + 2, SUB : SUB + cols, :] * own_weight
            for step in range(group)
            for comp in range(5)
        ]
        differences = jnp.dot(
            split(jnp.concatenate(lines, 0)), band[...], preferred_element_type=jnp.float32
        )
        for step in range(group):
            row = first + step
            state = [prim[comp, row] for comp in range(5)]
            flux = line_flux(state, enth[row])
            factor = height_wide[row]
            total = None
            for comp in range(5):
                start = (step * 5 + comp) * cols
                shift = lax.rem(target - (comp * rows + row) + LANES, LANES)
                difference = (
                    differences[start : start + cols]
                    + pltpu.roll(edge_recv[...], shift, 1) * edge_weight
                ) * factor
                normal[comp, row] = difference
                term = flux[comp] * difference
                total = term if total is None else total + term
            line_terms[row] = total
        return carry

    lax.fori_loop(0, rows // group, metric_rows, 0)
    every = jnp.dot(
        split(line_terms[...].reshape(rows * cols, LANES)),
        jnp.ones((2 * LANES, LANES), jnp.float32),
        preferred_element_type=jnp.float32,
    )
    sums = blank
    for row in range(rows):
        sums = jnp.where(lane == row, every[row * cols : row * cols + cols], sums)

    turn[...] = jnp.zeros_like(turn)
    turn[0:cols, :] = sums
    part_height = half_send[0, :, 0:cols] - turn[...].T[0:rows, 0:cols] / height_ref[...]
    tot_send[:, 0:cols] = jnp.sum(part_height, axis=0, keepdims=True)

    def total_copy(source, source_side, dest, dest_side):
        return pltpu.make_async_remote_copy(
            src_ref=tot_send,
            dst_ref=tot_recv.at[source_side * n_su + source],
            send_sem=tot_ssem.at[dest_side * n_su + dest],
            recv_sem=tot_rsem.at[source_side * n_su + source],
            device_id={"su": dest, "nrm": dest_side},
            device_id_type=MESH,
        )

    for other in range(n_su - 1):
        @pl.when(other < su)
        def _(other=other):
            for side in range(2):
                total_copy(su, nrm, other, side).start()

    half_send[0, :, 0:cols] = part_height
    half.start()

    @pl.when(sv > 0)
    def _():
        sv_up.wait_recv()

    @pl.when(sv < n_sv - 1)
    def _():
        sv_down.wait_recv()

    def unpack(row, carry):
        for comp in range(5):
            psi[comp, row + 2, SUB - 2 : SUB, :] = sv_recv[0, comp, row]
            psi[comp, row + 2, SUB + cols : SUB + cols + 2, :] = sv_recv[1, comp, row]
        rad_v[row, SUB - 2 : SUB, :] = sv_recv[0, 5, row]
        rad_v[row, SUB + cols : SUB + cols + 2, :] = sv_recv[1, 5, row]
        return carry

    lax.fori_loop(0, rows, unpack, 0, unroll=4)
    load_obj.wait()

    def residual_row(row, carry):
        for chunk in range(chunks):
            first = chunk * SUB
            part = slice(first, first + SUB)
            wide = slice(SUB + first, 2 * SUB + first)
            density, u1, u2, u3, pressure = [prim[comp, row, part, :] for comp in range(5)]
            enthalpy = enth[row, part, :]
            ru = [rad_u[row + offset, part, :] for offset in range(5)]
            rv = [rad_v[row, wide.start + offset - 2 : wide.stop + offset - 2, :] for offset in range(5)]
            ruv = 6.0 * (ru[2] + rv[2])
            g1, g2, damped = [], [], []
            for comp in range(5):
                centre = psi[comp, row + 2, wide, :]
                along = [psi[comp, row + offset, wide, :] for offset in (0, 1, 3, 4)]
                across = [
                    psi[comp, row + 2, wide.start + offset : wide.stop + offset, :]
                    for offset in (-2, -1, 1, 2)
                ]
                g1.append((along[1] - along[2]) * (2.0 / 3.0) - (along[0] - along[3]) * (1.0 / 12.0))
                g2.append((across[1] - across[2]) * (2.0 / 3.0) - (across[0] - across[3]) * (1.0 / 12.0))
                far = ru[0] * along[0] + ru[4] * along[3] + rv[0] * across[0] + rv[4] * across[3]
                near = ru[1] * along[1] + ru[3] * along[2] + rv[1] * across[1] + rv[3] * across[2]
                damped.append(far - 4.0 * near + ruv * centre)
            g3 = [normal[comp, row, part, :] for comp in range(5)]
            kinetic = (0.5 * gamma_less) * (u1 * u1 + u2 * u2 + u3 * u3)
            speeds = (u1, u2, u3)
            grads = (g1, g2, g3)
            spread = g1[1] + g2[2] + g3[3]
            energy = u1 * g1[4] + u2 * g2[4] + u3 * g3[4]
            carried = [u1 * g1[b] + u2 * g2[b] + u3 * g3[b] for b in (1, 2, 3)]
            shared = gamma_less * (spread + energy)
            out[0, row, part, :] = (
                out[0, row, part, :]
                + damped[0]
                + kinetic * spread
                - (u1 * carried[0] + u2 * carried[1] + u3 * carried[2])
                + (kinetic - enthalpy) * energy
            )
            for b in (1, 2, 3):
                g = grads[b - 1]
                dotted = u1 * g[1] + u2 * g[2] + u3 * g[3]
                out[b, row, part, :] = (
                    out[b, row, part, :]
                    + damped[b]
                    + carried[b - 1]
                    - speeds[b - 1] * shared
                    + (g[0] + dotted + enthalpy * g[4])
                )
            out[4, row, part, :] = (
                out[4, row, part, :] + damped[4] + gamma_less * spread + gamma_ratio * energy
            )
        return carry

    lax.fori_loop(2, rows - 2, residual_row, 0)

    @pl.when(su > 0)
    def _():
        psi_up.wait_recv()
        rad_up.wait_recv()

    @pl.when(su < n_su - 1)
    def _():
        psi_down.wait_recv()
        rad_down.wait_recv()

    lax.fori_loop(0, 2, residual_row, 0)
    lax.fori_loop(rows - 2, rows, residual_row, 0)

    half.wait_recv()
    summed = half_send[0, :, 0:cols] + half_recv[0, :, 0:cols]
    front_slope = half_send[1, :, 0:cols] + half_recv[1, :, 0:cols]
    step = 1
    while step < rows:
        summed = summed + jnp.concatenate(
            [summed[step:], jnp.zeros((step, cols), jnp.float32)], 0
        )
        step *= 2

    for other in range(1, n_su):
        @pl.when(other > su)
        def _(other=other):
            for side in range(2):
                total_copy(other, side, su, nrm).wait_recv()

    upstream = jnp.zeros((1, cols), jnp.float32)
    for other in range(n_su - 1, 0, -1):
        both = tot_recv[other, :, 0:cols] + tot_recv[n_su + other, :, 0:cols]
        upstream = upstream + jnp.where(other > su, both, 0.0)
    slope = (summed + upstream) * (1.0 / (rows * n_su)) + front_slope
    slope_ref[...] = slope
    turn[...] = jnp.zeros_like(turn)
    turn[0:rows, 0:cols] = slope
    slope_t[...] = turn[...].T[0:cols]

    @pl.when(su > 0)
    def _():
        psi_down.wait_send()
        rad_down.wait_send()

    @pl.when(su < n_su - 1)
    def _():
        psi_up.wait_send()
        rad_up.wait_send()

    @pl.when(sv > 0)
    def _():
        sv_down.wait_send()

    @pl.when(sv < n_sv - 1)
    def _():
        sv_up.wait_send()

    edge.wait_send()
    half.wait_send()
    for other in range(n_su - 1):
        @pl.when(other < su)
        def _(other=other):
            for side in range(2):
                total_copy(su, nrm, other, side).wait_send()


def finish_kernel(part_ref, prim, enth, slope_ref, slope_t, out_hbm, slope_hbm, out, sem, slope_sem):
    rows, cols = prim.shape[1], prim.shape[2]
    nrm = lax.axis_index("nrm")
    store_slope = pltpu.make_async_copy(slope_ref, slope_hbm, slope_sem)
    store_slope.start()
    lane = lax.broadcasted_iota(jnp.int32, (1, LANES), 1)
    fraction = ((nrm * LANES + lane).astype(jnp.float32) + 0.5) / (2 * LANES)
    group = 4

    def store(lap):
        where = pl.ds(lap * group, group)
        return pltpu.make_async_copy(out.at[:, where], out_hbm.at[:, where], sem.at[lap])

    for lap in range(rows // group):
        for row in range(lap * group, lap * group + group):
            column = jnp.broadcast_to(slope_t[:, row : row + 1], (cols, LANES))
            for chunk in range(cols // SUB):
                part = slice(chunk * SUB, chunk * SUB + SUB)
                state = [prim[comp, row, part, :] for comp in range(5)]
                flux = line_flux(state, enth[row, part, :])
                weight = column[part] * fraction
                for comp in range(5):
                    out[comp, row, part, :] = part_ref[comp, row, part, :] + weight * flux[comp]
        store(lap).start()
    for lap in range(rows // group):
        store(lap).wait()
    store_slope.wait()


def local(
    n_su, n_sv,
    primitive, adjoint_state, objective_grad, front_height,
    shock_state, state_by_height, state_by_slope, fitted_flags,
):
    _, rows, cols, depth = primitive.shape
    f32 = jnp.float32
    vmem = pl.BlockSpec(memory_space=pltpu.VMEM)
    block = (5, rows, cols, depth)
    wide = cols + 2 * SUB
    dma = pltpu.SemaphoreType.DMA
    operands = [
        pltpu.with_memory_space_constraint(operand, pltpu.HBM)
        for operand in (
            front_height, shock_state, state_by_height, state_by_slope, fitted_flags,
            primitive, adjoint_state, objective_grad,
        )
    ]
    small = (5, rows, cols)
    hbm = pl.BlockSpec(memory_space=pltpu.HBM)
    shape = jax.ShapeDtypeStruct
    held = pl.pallas_call(
        functools.partial(kernel, n_su, n_sv),
        out_shape=(
            shape(block, f32),
            shape(block, f32),
            shape((rows, cols, depth), f32),
            shape((rows, cols), f32),
            shape((cols, LANES), f32),
        ),
        in_specs=[hbm] * 8,
        out_specs=[vmem] * 5,
        scratch_shapes=[
            pltpu.VMEM((5, rows + 4, wide, depth), f32),
            pltpu.VMEM(block, f32),
            pltpu.VMEM((rows + 4, cols, depth), f32),
            pltpu.VMEM((rows, wide, depth), f32),
            pltpu.VMEM((rows, cols), f32),
            pltpu.VMEM(small, f32),
            pltpu.VMEM(small, f32),
            pltpu.VMEM(small, f32),
            pltpu.VMEM((rows, cols), jnp.int32),
            pltpu.VMEM((2, 6, rows, 2, depth), f32),
            pltpu.VMEM((2, 6, rows, 2, depth), f32),
            pltpu.VMEM((cols, LANES), f32),
            pltpu.VMEM((cols, LANES), f32),
            pltpu.VMEM((cols, LANES), f32),
            pltpu.VMEM((LANES, LANES), f32),
            pltpu.VMEM((cols, LANES), f32),
            pltpu.VMEM((rows, cols, LANES), f32),
            pltpu.VMEM((2 * LANES, LANES), f32),
            pltpu.VMEM((rows, cols, LANES), f32),
            pltpu.VMEM((2, rows, LANES), f32),
            pltpu.VMEM((2, rows, LANES), f32),
            pltpu.VMEM((1, LANES), f32),
            pltpu.VMEM((2 * n_su, 1, LANES), f32),
            dma((8,)),
            dma((8,)),
            dma((8,)),
            dma((2 * n_su,)),
            dma((2 * n_su,)),
        ],
        compiler_params=pltpu.CompilerParams(
            collective_id=0, has_side_effects=True, vmem_limit_bytes=24 * 1024 * 1024
        ),
    )(*operands)
    return pl.pallas_call(
        finish_kernel,
        out_shape=(shape(block, f32), shape((rows, cols), f32)),
        in_specs=[vmem] * 5,
        out_specs=(hbm, hbm),
        scratch_shapes=[pltpu.VMEM(block, f32), dma((rows // 4,)), dma],
        compiler_params=pltpu.CompilerParams(vmem_limit_bytes=16 * 1024 * 1024),
    )(*held)


def solution(mesh):
    assert mesh.shape["nrm"] == 2
    surface = P(None, "su", "sv")
    volume = P(None, "su", "sv", "nrm")
    return jax.shard_map(
        functools.partial(local, mesh.shape["su"], mesh.shape["sv"]),
        mesh=mesh,
        in_specs=(volume,) * 3 + (P("su", "sv"),) + (surface,) * 3 + (P("su", "sv"),),
        out_specs=(volume, P("su", "sv")),
        check_vma=False,
    )
```
